128 devices in a mesh: span: 8 (over y, x_hi), cross: 16 (over x_lo, z, core).
Axes of the slice: x: 4 (x_hi: 2, x_lo: 2; x = x_hi * 2 + x_lo), y: 4, z: 4, core: 2. Of those that a mesh axis runs over, the one named last changes fastest.
Arguments:
- adjoint_start: float32 [4, 128, 256, 1024], P(None, 'span', 'cross'), may hold values from -6 to 6
- base_flow: float32 [3, 128, 256, 1024], P(None, 'span', 'cross'), may hold values from -3 to 3
- wall_blocks: int32 [32768], P(('span', 'cross')), may hold values from 0 to 2047
- tile_sections: int32 [32768, 1], P(('span', 'cross')), may hold values from 0 to 255, as said below
- tile_normals: float32 [4, 32768], P(None, ('span', 'cross')), may hold values from -6 to 6
- modes: float32 [128, 128], replicated, may hold values from -0.5 to 0.5
Outputs:
- adjoint_field: float32 [4, 128, 256, 1024], P(None, 'span', 'cross')
- modal_load: float32 [256, 128], P(('span', 'cross'))
The draws below stay inside these ranges and needn't reach their ends.
Inputs may be any that keep to these rules, and one draw needn't show every extreme that they name: `tile_sections`: section s is owned by the device at flat index s // 2, span major. A tile names only sections whose owner has the tile's span index or one next to it. Among the tiles of one device, no section is named more than ceil(4) times, and that many on the devices at both span ends; every section is named by some tile.
All inputs are finite; a program needn't handle non-finite values.
Results may differ from the reference program's by a relative error of at most 0.00012.
Values sent between devices are 32-bit elements; how exact they have to be, the bound alone decides.
No kernel may reach another device: no remote copies, remote signals or barrier semaphores. Data moves between devices by JAX's collectives and lax.ppermute only.
A program may use at most 128 MiB of HBM per device.

```python
import jax
import jax.numpy as jnp
from jax import lax

NX = 1024
CY = 16
CZ = 16
STEPS = 3
TILES_DEV = 256
SEC_DEV = 2
MODES = 128
NZ = 128
NY = 256
TILES = 32768
N_SPAN = 8
N_CROSS = 16


def draw_tile_sections(key, part):
    key = jax.random.fold_in(key, 11)
    per_span = N_CROSS * SEC_DEV
    device = jnp.arange(N_SPAN * N_CROSS, dtype=jnp.int32)
    span_idx = device // N_CROSS
    cross_idx = device % N_CROSS
    lowest = jnp.maximum(span_idx - 1, 0)
    highest = jnp.minimum(span_idx + 1, N_SPAN - 1)
    choices_count = (highest - lowest + 1) * per_span
    rotate = jax.random.randint(jax.random.fold_in(key, 1), (N_SPAN,), 0, 3 * per_span, dtype=jnp.int32)
    keys = jax.random.split(jax.random.fold_in(key, 2), N_SPAN * N_CROSS)
    orders = jax.vmap(lambda k: jax.random.permutation(k, TILES_DEV))(keys).astype(jnp.int32)
    slot = (cross_idx[:, None] * TILES_DEV + orders + rotate[span_idx][:, None]) % choices_count[:, None]
    section = lowest[:, None] * per_span + slot
    return section.reshape(TILES_DEV * N_SPAN * N_CROSS, 1).astype(jnp.int32)


def touch_ends(values, rng, least, largest):
    longest = values.shape.index(max(values.shape))
    spots = []
    for shift in (0, 1):
        where = [jax.random.randint(jax.random.fold_in(rng, axis), (), 0, length) for axis, length in enumerate(values.shape)]
        where[longest] = (where[longest] + shift) % values.shape[longest]
        spots.append(tuple(where))
    return values.at[spots[0]].set(least).at[spots[1]].set(largest)


def level_of(own_key, shape, pieces, low, high):
    factor_of = 1.0
    for position, shards_of in pieces:
        heights = jax.random.uniform(jax.random.fold_in(jax.random.fold_in(own_key, 6), position), (shards_of,), jnp.float32, low / len(pieces), high / len(pieces))
        factor_of = factor_of * jnp.repeat(jnp.exp(heights), shape[position] // shards_of).reshape((-1,) + (1,) * (len(shape) - 1 - position))
    return factor_of


def noise(own_key, shape, width, reach, cuts=(), kind=jnp.bfloat16):
    drawn = width * jax.random.normal(own_key, shape, jnp.float32)
    if cuts:
        drawn = drawn * level_of(own_key, shape, cuts, -0.22, 0.18)
    return jnp.clip(drawn, -reach, reach).astype(kind)


def setup_inputs(seed: int = 0) -> dict:
    streams_of = jax.random.split(jax.random.key(seed), 7)
    adjoint_start = noise(streams_of[0], (4, NZ, NY, NX), 1.0, 6.0, ((1, 8), (2, 16)), jnp.float32)
    base_flow = noise(streams_of[1], (3, NZ, NY, NX), 0.5, 3.0, ((1, 8), (2, 16)), jnp.float32)
    wall_blocks = touch_ends(jax.random.randint(streams_of[2], (TILES,), 0, CZ * CY * NX // 128), jax.random.fold_in(streams_of[2], 1), 0, (CZ * CY * NX // 128) - 1).astype(jnp.int32)
    tile_sections = draw_tile_sections(jax.random.fold_in(streams_of[6], 71), 0)
    tile_normals = noise(streams_of[4], (4, TILES), 1.0, 6.0, ((1, 128),), jnp.float32)
    modes = noise(streams_of[5], (128, MODES), 128 ** -0.5, 0.5, (), jnp.float32)
    return dict(adjoint_start=adjoint_start, base_flow=base_flow, wall_blocks=wall_blocks, tile_sections=tile_sections, tile_normals=tile_normals, modes=modes)


time_step = 0.25
viscosity = 0.1


def derivs(padded):
    center = padded[:, 1:-1, 1:-1, :]
    along_z = (padded[:, 2:, 1:-1, :] - padded[:, :-2, 1:-1, :]) * 0.5
    along_y = (padded[:, 1:-1, 2:, :] - padded[:, 1:-1, :-2, :]) * 0.5
    xpad = jnp.pad(center, ((0, 0), (0, 0), (0, 0), (1, 1)))
    along_x = (xpad[..., 2:] - xpad[..., :-2]) * 0.5
    lapl = xpad[..., 2:] + xpad[..., :-2] + padded[:, 2:, 1:-1, :] + padded[:, :-2, 1:-1, :]
    lapl = lapl + padded[:, 1:-1, 2:, :] + padded[:, 1:-1, :-2, :] - 6.0 * center
    return center, (along_x, along_y, along_z), lapl


def advance(padded, base, grads):
    field, diffs, lapl = derivs(padded)
    result = []
    for comp in range(3):
        advect = base[0] * diffs[0][comp] + base[1] * diffs[1][comp] + base[2] * diffs[2][comp]
        coupled = grads[comp][0] * field[0] + grads[comp][1] * field[1] + grads[comp][2] * field[2]
        result.append(field[comp] + time_step * (advect - coupled - diffs[comp][3] + viscosity * lapl[comp]))
    diverg = diffs[0][0] + diffs[1][1] + diffs[2][2]
    result.append(field[3] - time_step * diverg)
    return jnp.stack(result)


def pad_zy(field):
    return jnp.pad(field, ((0, 0), (1, 1), (1, 1), (0, 0)))


def reference(adjoint_start, base_flow, wall_blocks, tile_sections, tile_normals, modes):
    blocks_x = NX // 128
    base_pad = pad_zy(base_flow)
    center, bdiff, blap = derivs(base_pad)
    grads = [[bdiff[i][j] for j in range(3)] for i in range(3)]
    count = TILES_DEV * N_SPAN * N_CROSS
    flat = jnp.arange(count, dtype=jnp.int32)
    device = flat // TILES_DEV
    span_idx = device // N_CROSS
    cross_idx = device % N_CROSS
    zl = wall_blocks // (CY * blocks_x)
    yl = (wall_blocks // blocks_x) % CY
    xb = wall_blocks % blocks_x
    zg = (span_idx * CZ + zl).astype(jnp.int32)
    yg = (cross_idx * CY + yl).astype(jnp.int32)
    field = adjoint_start
    rows_sum = jnp.zeros((count, 128), jnp.float32)
    for step in range(STEPS):
        field = advance(pad_zy(field), base_flow, grads)
        shaped = field.reshape(4, NZ, NY, blocks_x, 128)
        rows = shaped[:, zg, yg, xb]
        trac = jnp.sum(tile_normals[:, :, None] * rows, axis=0)
        rows_sum = rows_sum + time_step * trac
    section_sum = jax.ops.segment_sum(rows_sum, tile_sections[:, 0], num_segments=SEC_DEV * N_SPAN * N_CROSS)
    modal_load = jnp.dot(section_sum, modes, precision=lax.Precision.HIGHEST, preferred_element_type=jnp.float32)
    return field, modal_load
```

```python
import functools

import jax
import jax.numpy as jnp
from jax import lax
from jax.experimental import pallas as pl
from jax.experimental.pallas import tpu as pltpu
from jax.sharding import PartitionSpec as P

STEPS = 3
SEC_DEV = 2
TIME_STEP = 0.25
VISCOSITY = 0.1
LANES = 128
ROWS = 8
HALF = 0.5 * TIME_STEP
DIFF = TIME_STEP * VISCOSITY
KEEP = 1.0 - 6.0 * DIFF

VMEM = pltpu.VMEM
SMEM = pltpu.SMEM


def lane_shifts(get, k, last, lane):
    here = get(k)
    plus = pltpu.roll(here, LANES - 1, 1)
    minus = pltpu.roll(here, 1, 1)
    next_one = pltpu.roll(get(k + 1), LANES - 1, 1) if k < last else 0.0
    prev_one = pltpu.roll(get(k - 1), 1, 1) if k > 0 else 0.0
    return jnp.where(lane == LANES - 1, next_one, plus), jnp.where(lane == 0, prev_one, minus)


def row_shifts(tiles, yt, halo_lo, halo_hi, sub):
    here = tiles[yt]
    plus = pltpu.roll(here, ROWS - 1, 0)
    minus = pltpu.roll(here, 1, 0)
    if yt + 1 < len(tiles):
        over = pltpu.roll(tiles[yt + 1], ROWS - 1, 0)
    else:
        over = jnp.broadcast_to(halo_hi, here.shape)
    if yt > 0:
        under = pltpu.roll(tiles[yt - 1], 1, 0)
    else:
        under = jnp.broadcast_to(halo_lo, here.shape)
    return jnp.where(sub == ROWS - 1, over, plus), jnp.where(sub == 0, under, minus)


def plane(field, field_lo, field_hi, base, base_lo, base_hi, y_lo, y_hi, put, ny, nx):
    lane = lax.broadcasted_iota(jnp.int32, (ROWS, LANES), 1)
    sub = lax.broadcasted_iota(jnp.int32, (ROWS, LANES), 0)
    last = nx // LANES - 1
    tiles = ny // ROWS
    for k in range(nx // LANES):
        for yt in range(tiles):
            def around(get, off, c):
                xs = lane_shifts(lambda kk: get(c, yt, kk), k, last, lane)
                ys = row_shifts([get(c, j, k) for j in range(tiles)], yt, y_lo(off + c, k), y_hi(off + c, k), sub)
                return xs, ys
            f = [field(c, yt, k) for c in range(4)]
            u = [base(c, yt, k) for c in range(3)]
            fs, us = [], []
            for c in range(4):
                xs, ys = around(field, 0, c)
                fs.append((xs, ys, (field_hi(c, yt, k), field_lo(c, yt, k))))
            for c in range(3):
                xs, ys = around(base, 4, c)
                us.append((xs, ys, (base_hi(c, yt, k), base_lo(c, yt, k))))
            scaled = [HALF * u[d] for d in range(3)]
            up = [scaled[d] + DIFF for d in range(3)]
            down = [DIFF - scaled[d] for d in range(3)]
            out = []
            for i in range(3):
                acc = KEEP * f[i]
                for d in range(3):
                    acc = acc + up[d] * fs[i][d][0] + down[d] * fs[i][d][1]
                pull = fs[3][i][0] - fs[3][i][1]
                for j in range(3):
                    pull = pull + (us[j][i][0] - us[j][i][1]) * f[j]
                out.append(acc - HALF * pull)
            div = fs[0][0][0] - fs[0][0][1]
            for d in (1, 2):
                div = div + (fs[d][d][0] - fs[d][d][1])
            out.append(f[3] - HALF * div)
            for c in range(4):
                put(c, yt, k, out[c])


def tile_of(ref, index):
    def get(c, yt, k):
        return ref[(c, *index, pl.ds(yt * ROWS, ROWS), pl.ds(k * LANES, LANES))]
    return get


def pack_kernel(field, base, z_lo, z_hi, y_lo, y_hi, sems):
    nz, ny, nx = field.shape[1:]
    copies = []
    for src, lo, hi in ((field, 0, 4), (base, 4, 7)):
        copies += [(src.at[:, 0], z_lo.at[lo:hi]), (src.at[:, nz - 1], z_hi.at[lo:hi])]
        for k in range(nx // LANES):
            col = pl.ds(k * LANES, LANES)
            copies += [
                (src.at[:, :, 0, col], y_lo.at[lo:hi, :, k]),
                (src.at[:, :, ny - 1, col], y_hi.at[lo:hi, :, k]),
            ]
    started = [pltpu.make_async_copy(a, b, sems.at[i]) for i, (a, b) in enumerate(copies)]
    for one in started:
        one.start()
    for one in started:
        one.wait()


def pack(field, base):
    _, nz, ny, nx = field.shape
    per_row = nx // LANES
    shapes = [(7, ny, nx), (7, ny, nx), (7, nz, per_row, LANES), (7, nz, per_row, LANES)]
    return pl.pallas_call(
        pack_kernel,
        out_shape=[jax.ShapeDtypeStruct(s, jnp.float32) for s in shapes],
        in_specs=[pl.BlockSpec(memory_space=pl.ANY)] * 2,
        out_specs=[pl.BlockSpec(memory_space=pl.ANY)] * 4,
        scratch_shapes=[pltpu.SemaphoreType.DMA((4 + 4 * per_row,))],
        name="pack_faces",
    )(field, base)


def step_kernel(first, field, base, zf_lo, zf_hi, yf_lo, yf_hi, zb_lo, zb_hi, yb_lo, yb_hi, blocks, normals, rows_in,
                new, z_lo, z_hi, y_lo, y_hi, rows):
    _, nz, ny, nx = field.shape
    boff = zb_lo.shape[0] - 3

    def do(z, f_lo, f_hi, b_lo, b_hi):
        def halo(fref, bref):
            def get(c, k):
                if c < 4:
                    return fref[c, z, pl.ds(k, 1), :]
                return bref[boff + c - 4, z, pl.ds(k, 1), :]
            return get

        def put(c, yt, k, value):
            col = pl.ds(k * LANES, LANES)
            new[c, z, pl.ds(yt * ROWS, ROWS), col] = value
            if yt == 0:
                y_lo[c, z, pl.ds(k, 1), :] = value[:1]
            if yt == ny // ROWS - 1:
                y_hi[c, z, pl.ds(k, 1), :] = value[ROWS - 1:]

        plane(tile_of(field, (z,)), f_lo, f_hi, tile_of(base, (z,)), b_lo, b_hi, halo(yf_lo, yb_lo), halo(yf_hi, yb_hi), put, ny, nx)

    def shifted(ref, off):
        inner = tile_of(ref, ())
        return lambda c, yt, k: inner(c + off, yt, k)

    do(0, shifted(zf_lo, 0), tile_of(field, (1,)), shifted(zb_lo, boff), tile_of(base, (1,)))

    def body(z, carry):
        do(z, tile_of(field, (z - 1,)), tile_of(field, (z + 1,)), tile_of(base, (z - 1,)), tile_of(base, (z + 1,)))
        return carry

    lax.fori_loop(1, nz - 1, body, 0)
    do(nz - 1, tile_of(field, (nz - 2,)), shifted(zf_hi, 0), tile_of(base, (nz - 2,)), shifted(zb_hi, boff))
    z_lo[...] = new[:, 0]
    z_hi[...] = new[:, nz - 1]

    per_row = nx // LANES

    row_bits, y_bits = per_row.bit_length() - 1, ny.bit_length() - 1
    sub = lax.broadcasted_iota(jnp.int32, (ROWS, LANES), 0)

    def gather(group, carry):
        kept = jnp.zeros((ROWS, LANES), jnp.float32)
        for j in range(ROWS):
            t = group * ROWS + j
            b = blocks[t]
            z = lax.shift_right_logical(b, row_bits + y_bits)
            y = lax.shift_right_logical(b, row_bits) & (ny - 1)
            near = pl.ds(pl.multiple_of(y & (ny - ROWS), ROWS), ROWS)
            col = pl.ds(pl.multiple_of((b & (per_row - 1)) * LANES, LANES), LANES)
            total = normals[0, t] * new[0, z, near, col]
            for c in range(1, 4):
                total = total + normals[c, t] * new[c, z, near, col]
            total = pltpu.roll(total, (j + ROWS - (y & (ROWS - 1))) & (ROWS - 1), 0)
            kept = jnp.where(sub == j, total, kept)
        kept = TIME_STEP * kept
        here = pl.ds(pl.multiple_of(group * ROWS, ROWS), ROWS)
        if not first:
            kept = kept + rows_in[here, :]
        rows[here, :] = kept
        return carry

    lax.fori_loop(0, rows.shape[0] // ROWS, gather, 0)


def advance(first, field, base, halos, base_halos, blocks, normals, rows):
    _, nz, ny, nx = field.shape
    per_row = nx // LANES
    shapes = [field.shape, (4, ny, nx), (4, ny, nx), (4, nz, per_row, LANES), (4, nz, per_row, LANES), rows.shape]
    vm = pl.BlockSpec(memory_space=VMEM)
    sm = pl.BlockSpec(memory_space=SMEM)
    return pl.pallas_call(
        functools.partial(step_kernel, first),
        out_shape=[jax.ShapeDtypeStruct(s, jnp.float32) for s in shapes],
        in_specs=[vm] * 10 + [sm, sm, vm],
        out_specs=[vm] * 6,
        compiler_params=pltpu.CompilerParams(vmem_limit_bytes=48 * 2**20),
        name="adjoint_step",
    )(field, base, *halos, *base_halos, blocks, normals, rows)


def shift_along(block, axis, distance):
    count = lax.axis_size(axis)
    route = [(i, i + distance) for i in range(count) if 0 <= i + distance < count]
    return lax.ppermute(block, axis, route)


def exchange(z_lo, z_hi, y_lo, y_hi):
    return (shift_along(z_hi, "span", 1), shift_along(z_lo, "span", -1),
            shift_along(y_hi, "cross", 1), shift_along(y_lo, "cross", -1))


def local(adjoint_start, base_flow, wall_blocks, tile_sections, tile_normals, modes):
    halos = exchange(*pack(adjoint_start, base_flow))
    base_halos = halos
    field = adjoint_start
    rows = jnp.zeros((wall_blocks.shape[0], LANES), jnp.float32)
    for step in range(STEPS):
        field, *faces, rows = advance(step == 0, field, base_flow, halos, base_halos, wall_blocks, tile_normals, rows)
        if step < STEPS - 1:
            halos = exchange(*faces)
    crosses = lax.axis_size("cross")
    per_span = SEC_DEV * crosses
    relative = tile_sections[:, 0] - (lax.axis_index("span") - 1) * per_span
    span_off, inside = relative // per_span, relative % per_span
    spot = (inside // SEC_DEV) * (3 * SEC_DEV) + span_off * SEC_DEV + inside % SEC_DEV
    labels = jnp.arange(3 * per_span, dtype=jnp.int32)
    onehot = (spot[None, :] == labels[:, None]).astype(jnp.float32)
    table = jnp.dot(onehot, rows, precision=lax.Precision.HIGHEST, preferred_element_type=jnp.float32)
    parts = lax.all_to_all(table.reshape(crosses, 3 * SEC_DEV, LANES), "cross", 0, 0, tiled=True)
    reduced = jnp.sum(parts, axis=0)
    above = shift_along(reduced[:SEC_DEV], "span", -1)
    below = shift_along(reduced[2 * SEC_DEV:], "span", 1)
    section_sum = reduced[SEC_DEV:2 * SEC_DEV] + above + below
    modal_load = jnp.dot(section_sum, modes, precision=lax.Precision.HIGHEST, preferred_element_type=jnp.float32)
    return field, modal_load


def solution(mesh):
    placed = (
        P(None, "span", "cross", None),
        P(None, "span", "cross", None),
        P(("span", "cross")),
        P(("span", "cross"), None),
        P(None, ("span", "cross")),
        P(),
    )
    return jax.shard_map(
        local,
        mesh=mesh,
        in_specs=placed,
        out_specs=(P(None, "span", "cross", None), P(("span", "cross"), None)),
        check_vma=False,
    )
```

```python
import functools

import jax
import jax.numpy as jnp
from jax import lax
from jax.experimental import pallas as pl
from jax.experimental.pallas import tpu as pltpu
from jax.sharding import PartitionSpec as P

STEPS = 3
SEC_DEV = 2
TIME_STEP = 0.25
VISCOSITY = 0.1
LANES = 128
ROWS = 8
HALF = 0.5 * TIME_STEP
DIFF = TIME_STEP * VISCOSITY
KEEP = 1.0 - 6.0 * DIFF

VMEM = pltpu.VMEM
SMEM = pltpu.SMEM


def lane_shifts(get, k, last, lane):
    here = get(k)
    plus = pltpu.roll(here, LANES - 1, 1)
    minus = pltpu.roll(here, 1, 1)
    next_one = pltpu.roll(get(k + 1), LANES - 1, 1) if k < last else 0.0
    prev_one = pltpu.roll(get(k - 1), 1, 1) if k > 0 else 0.0
    return jnp.where(lane == LANES - 1, next_one, plus), jnp.where(lane == 0, prev_one, minus)


def row_shifts(tiles, yt, sub):
    here = tiles[yt]
    plus = pltpu.roll(here, ROWS - 1, 0)
    minus = pltpu.roll(here, 1, 0)
    over = pltpu.roll(tiles[yt + 1], ROWS - 1, 0) if yt + 1 < len(tiles) else 0.0
    under = pltpu.roll(tiles[yt - 1], 1, 0) if yt > 0 else 0.0
    return jnp.where(sub == ROWS - 1, over, plus), jnp.where(sub == 0, under, minus)


def plane(field, field_lo, field_hi, base, base_lo, base_hi, put, ny, nx):
    lane = lax.broadcasted_iota(jnp.int32, (ROWS, LANES), 1)
    sub = lax.broadcasted_iota(jnp.int32, (ROWS, LANES), 0)
    last = nx // LANES - 1
    tiles = ny // ROWS
    for k in range(nx // LANES):
        for yt in range(tiles):
            def around(get, get_lo, get_hi, c):
                xs = lane_shifts(lambda kk: get(c, yt, kk), k, last, lane)
                ys = row_shifts([get(c, j, k) for j in range(tiles)], yt, sub)
                return xs, ys, (get_hi(c, yt, k), get_lo(c, yt, k))
            f = [field(c, yt, k) for c in range(4)]
            u = [base(c, yt, k) for c in range(3)]
            fs = [around(field, field_lo, field_hi, c) for c in range(4)]
            us = [around(base, base_lo, base_hi, c) for c in range(3)]
            scaled = [HALF * u[d] for d in range(3)]
            up = [scaled[d] + DIFF for d in range(3)]
            down = [DIFF - scaled[d] for d in range(3)]
            out = []
            for i in range(3):
                acc = KEEP * f[i]
                for d in range(3):
                    acc = acc + up[d] * fs[i][d][0] + down[d] * fs[i][d][1]
                pull = fs[3][i][0] - fs[3][i][1]
                for j in range(3):
                    pull = pull + (us[j][i][0] - us[j][i][1]) * f[j]
                out.append(acc - HALF * pull)
            div = fs[0][0][0] - fs[0][0][1]
            for d in (1, 2):
                div = div + (fs[d][d][0] - fs[d][d][1])
            out.append(f[3] - HALF * div)
            for c in range(4):
                put(c, yt, k, out[c])


def fix(sign, d, f, u, beyond_f, beyond_u):
    coef = DIFF + (sign * HALF) * u[d]
    out = [coef * beyond_f[i] for i in range(3)]
    pull = beyond_f[3]
    for j in range(3):
        pull = pull + beyond_u[j] * f[j]
    out[d] = out[d] - (sign * HALF) * pull
    return out + [(-sign * HALF) * beyond_f[d]]


def tile_of(ref, index):
    def get(c, yt, k):
        return ref[(c, *index, pl.ds(yt * ROWS, ROWS), pl.ds(k * LANES, LANES))]
    return get


def pack_kernel(field, base, z_lo, z_hi, y_lo, y_hi):
    nz, ny, nx = field.shape[1:]

    def body(z, carry):
        for src, off, n in ((field, 0, 4), (base, 4, 3)):
            for c in range(n):
                for k in range(nx // LANES):
                    col = pl.ds(k * LANES, LANES)
                    y_lo[c + off, z, pl.ds(k, 1), :] = src[c, z, pl.ds(0, 1), col]
                    y_hi[c + off, z, pl.ds(k, 1), :] = src[c, z, pl.ds(ny - 1, 1), col]
        return carry

    lax.fori_loop(0, nz, body, 0)
    z_lo[0:4] = field[:, 0]
    z_lo[4:7] = base[:, 0]
    z_hi[0:4] = field[:, nz - 1]
    z_hi[4:7] = base[:, nz - 1]


def f32(*shape):
    return jax.ShapeDtypeStruct(shape, jnp.float32)


def call(kernel, name, out_shape, in_specs, out_specs, scratch=(), mib=20, cost=None):
    return pl.pallas_call(
        kernel,
        out_shape=out_shape,
        in_specs=in_specs,
        out_specs=out_specs,
        scratch_shapes=list(scratch),
        compiler_params=pltpu.CompilerParams(vmem_limit_bytes=mib * 2**20),
        cost_estimate=cost,
        name=name,
    )


IN_VMEM = pl.BlockSpec(memory_space=VMEM)
IN_SMEM = pl.BlockSpec(memory_space=SMEM)
ANYWHERE = pl.BlockSpec(memory_space=pl.ANY)


def pack(field, base):
    _, nz, ny, nx = field.shape
    shapes = [f32(7, ny, nx)] * 2 + [f32(7, nz, nx // LANES, LANES)] * 2
    return call(pack_kernel, "pack_faces", shapes, [IN_VMEM] * 2, [IN_VMEM] * 4)(field, base)


def gather_tiles(cells, z_off, blocks, normals, rows, rows_in):
    ny, nx = cells.shape[2:]
    per_row = nx // LANES
    row_bits, y_bits = per_row.bit_length() - 1, ny.bit_length() - 1
    sub = lax.broadcasted_iota(jnp.int32, (ROWS, LANES), 0)

    def gather(group, carry):
        kept = jnp.zeros((ROWS, LANES), jnp.float32)
        for j in range(ROWS):
            t = group * ROWS + j
            b = blocks[t]
            z = lax.shift_right_logical(b, row_bits + y_bits) + z_off
            y = lax.shift_right_logical(b, row_bits) & (ny - 1)
            near = pl.ds(pl.multiple_of(y & (ny - ROWS), ROWS), ROWS)
            col = pl.ds(pl.multiple_of((b & (per_row - 1)) * LANES, LANES), LANES)
            total = normals[0, t] * cells[0, z, near, col]
            for c in range(1, 4):
                total = total + normals[c, t] * cells[c, z, near, col]
            total = pltpu.roll(total, (j + ROWS - (y & (ROWS - 1))) & (ROWS - 1), 0)
            kept = jnp.where(sub == j, total, kept)
        kept = TIME_STEP * kept
        here = pl.ds(pl.multiple_of(group * ROWS, ROWS), ROWS)
        if rows_in is not None:
            kept = kept + rows_in[here, :]
        rows[here, :] = kept
        return carry

    lax.fori_loop(0, rows.shape[0] // ROWS, gather, 0)


def put_rows(cells, at, rows_lo, rows_hi, z):
    ny, nx = cells.shape[2:]
    for c in range(4):
        for k in range(nx // LANES):
            col = pl.ds(k * LANES, LANES)
            cells[c, at, pl.ds(0, 1), col] = rows_lo[c, z, pl.ds(k, 1), :]
            cells[c, at, pl.ds(ny - 1, 1), col] = rows_hi[c, z, pl.ds(k, 1), :]


def stencil_kernel(step, *refs):
    if step == 0:
        (field, base, new, p_lo, p_hi, r_lo, r_hi, cells, flow, fresh, fsem, usem, osem) = refs
    else:
        (field, base, own_lo, own_hi, row_lo, row_hi, blocks, normals, *rest) = refs
        if step > 1:
            rows_in, *rest = rest
        else:
            rows_in = None
        (new, p_lo, p_hi, r_lo, r_hi, rows, cells, flow, fresh, fsem, usem, osem) = rest
    nz, ny, nx = fresh.shape[1:]

    def load(z):
        return (pltpu.make_async_copy(field.at[:, z], cells.at[:, z + 1], fsem.at[z]),
                pltpu.make_async_copy(base.at[:, z], flow.at[:, z + 1], usem.at[z]))

    def store(z):
        return pltpu.make_async_copy(fresh.at[:, z], new.at[:, z], osem.at[z])

    def start(z, carry):
        for one in load(z):
            one.start()
        return carry

    lax.fori_loop(0, nz, start, 0)
    for at in (0, nz + 1):
        cells[:, at] = jnp.zeros((4, ny, nx), jnp.float32)
        flow[:, at] = jnp.zeros((3, ny, nx), jnp.float32)

    def ready(z):
        for one in load(z):
            one.wait()
        if step > 0:
            put_rows(cells, z + 1, row_lo, row_hi, z)

    ready(0)
    if step > 0:
        cells[:, 1] = own_lo[...]

    def body(z, carry):
        @pl.when(z + 1 < nz)
        def _():
            ready(z + 1)

        if step > 0:
            @pl.when(z + 1 == nz - 1)
            def _():
                cells[:, nz] = own_hi[...]

        def put(c, yt, k, value):
            fresh[c, z, pl.ds(yt * ROWS, ROWS), pl.ds(k * LANES, LANES)] = value
            if yt == 0:
                r_lo[c, z, pl.ds(k, 1), :] = value[:1]
            if yt == ny // ROWS - 1:
                r_hi[c, z, pl.ds(k, 1), :] = value[ROWS - 1:]

        plane(tile_of(cells, (z + 1,)), tile_of(cells, (z,)), tile_of(cells, (z + 2,)),
              tile_of(flow, (z + 1,)), tile_of(flow, (z,)), tile_of(flow, (z + 2,)), put, ny, nx)
        store(z).start()
        return carry

    lax.fori_loop(0, nz, body, 0)
    p_lo[...] = fresh[:, 0]
    p_hi[...] = fresh[:, nz - 1]
    if step > 0:
        gather_tiles(cells, 1, blocks, normals, rows, rows_in)

    def finish(z, carry):
        store(z).wait()
        return carry

    lax.fori_loop(0, nz, finish, 0)


def stencil(step, field, base, own=(), rows=(), blocks=None, normals=None, rows_in=()):
    _, nz, ny, nx = field.shape
    per_row = nx // LANES
    outs = [f32(*field.shape)] + [f32(4, ny, nx)] * 2 + [f32(4, nz, per_row, LANES)] * 2
    specs = [ANYWHERE] + [IN_VMEM] * 4
    ins, args = [ANYWHERE] * 2, [field, base]
    if step > 0:
        ins += [IN_VMEM] * 4 + [IN_SMEM] * 2 + [IN_VMEM] * len(rows_in)
        args += [*own, *rows, blocks, normals, *rows_in]
        outs.append(f32(blocks.shape[0], LANES))
        specs.append(IN_VMEM)
    scratch = [VMEM((4, nz + 2, ny, nx), jnp.float32), VMEM((3, nz + 2, ny, nx), jnp.float32), VMEM((4, nz, ny, nx), jnp.float32)]
    scratch += [pltpu.SemaphoreType.DMA((nz,))] * 3
    cost = pl.CostEstimate(flops=130 * field.size // 4, bytes_accessed=11 * 2**20, transcendentals=0)
    return call(functools.partial(stencil_kernel, step), "stencil", outs, ins, specs, scratch, 32, cost)(*args)


def row_fix_kernel(p_lo, p_hi, r_lo, r_hi, own_lo, own_hi, base_lo, base_hi, far_lo, far_hi, fbase_lo, fbase_hi,
                   q_lo, q_hi, s_lo, s_hi):
    _, ny, nx = p_lo.shape
    nz = r_lo.shape[1]

    def body(z, carry):
        for sign, r, own, base, far, fbase, s in ((-1, r_lo, own_lo, base_lo, far_lo, fbase_lo, s_lo),
                                                  (1, r_hi, own_hi, base_hi, far_hi, fbase_hi, s_hi)):
            add = fix(sign, 1, [own[c, z] for c in range(3)], [base[4 + c, z] for c in range(3)],
                      [far[c, z] for c in range(4)], [fbase[4 + c, z] for c in range(3)])
            for c in range(4):
                s[c, z] = r[c, z] + add[c]
        return carry

    lax.fori_loop(0, nz, body, 0)
    for z, p, q in ((0, p_lo, q_lo), (nz - 1, p_hi, q_hi)):
        q[...] = p[...]
        for c in range(4):
            for k in range(nx // LANES):
                col = pl.ds(k * LANES, LANES)
                q[c, pl.ds(0, 1), col] = s_lo[c, z, pl.ds(k, 1), :]
                q[c, pl.ds(ny - 1, 1), col] = s_hi[c, z, pl.ds(k, 1), :]


def row_fix(planes, rows, own_rows, base_rows, far_rows, far_base_rows):
    outs = [f32(*planes[0].shape)] * 2 + [f32(*rows[0].shape)] * 2
    cost = pl.CostEstimate(flops=10**6, bytes_accessed=2**18, transcendentals=0)
    return call(row_fix_kernel, "row_fix", outs, [IN_VMEM] * 12, [IN_VMEM] * 4, cost=cost)(
        *planes, *rows, *own_rows, *base_rows, *far_rows, *far_base_rows)


def plane_fix_kernel(first, *refs):
    (q_lo, q_hi, s_lo, s_hi, own_lo, own_hi, base_lo, base_hi, fbase_lo, fbase_hi, far_lo, far_hi, *rest) = refs
    if first:
        out_lo, out_hi, row_lo, row_hi = rest
    else:
        old_lo, old_hi, got_lo, got_hi, out_lo, out_hi, row_lo, row_hi, next_lo, next_hi = rest
    _, ny, nx = q_lo.shape
    nz = s_lo.shape[1]
    span = lax.axis_index("span")
    sides = (
        (-1, q_lo, own_lo, base_lo, fbase_lo, far_lo, out_lo, span > 0),
        (1, q_hi, own_hi, base_hi, fbase_hi, far_hi, out_hi, span < lax.axis_size("span") - 1),
    )
    for side, (sign, q, own, base, fbase, far, out, there) in enumerate(sides):
        for yt in range(ny // ROWS):
            for k in range(nx // LANES):
                tile = (pl.ds(yt * ROWS, ROWS), pl.ds(k * LANES, LANES))
                u = [base[(4 + c, *tile)] for c in range(3)]
                fu = [fbase[(4 + c, *tile)] for c in range(3)]
                beyond = [far[(c, *tile)] for c in range(4)]
                if not first:
                    old, got, nxt = ((old_lo, got_lo, next_lo), (old_hi, got_hi, next_hi))[side]
                    back = fix(-sign, 2, beyond, fu, [old[(c, *tile)] for c in range(4)], u)
                    beyond = [jnp.where(there, got[(c, *tile)] + back[c], 0.0) for c in range(4)]
                    for c in range(4):
                        nxt[(c, *tile)] = beyond[c]
                add = fix(sign, 2, [own[(c, *tile)] for c in range(3)], u, beyond, fu)
                for c in range(4):
                    out[(c, *tile)] = q[(c, *tile)] + add[c]
    row_lo[...] = s_lo[...]
    row_hi[...] = s_hi[...]
    for z, out in ((0, out_lo), (nz - 1, out_hi)):
        for c in range(4):
            for k in range(nx // LANES):
                col = pl.ds(k * LANES, LANES)
                row_lo[c, z, pl.ds(k, 1), :] = out[c, pl.ds(0, 1), col]
                row_hi[c, z, pl.ds(k, 1), :] = out[c, pl.ds(ny - 1, 1), col]


def plane_fix(planes, rows, own, base, far_base, far, old=(), got=()):
    first = not got
    outs = [f32(*planes[0].shape)] * 2 + [f32(*rows[0].shape)] * 2
    if not first:
        outs += [f32(*planes[0].shape)] * 2
    cost = pl.CostEstimate(flops=10**6, bytes_accessed=2**18, transcendentals=0)
    args = [*planes, *rows, *own, *base, *far_base, *far, *old, *got]
    return call(functools.partial(plane_fix_kernel, first), "plane_fix", outs, [IN_VMEM] * len(args), [IN_VMEM] * len(outs),
                cost=cost)(*args)


def finish_kernel(field, own_lo, own_hi, row_lo, row_hi, blocks, normals, sections, rows_in, new, table, cells, rows, fsem, osem):
    nz, ny, nx = cells.shape[1:]

    def load(z):
        return pltpu.make_async_copy(field.at[:, z], cells.at[:, z], fsem.at[z])

    def store(z):
        return pltpu.make_async_copy(cells.at[:, z], new.at[:, z], osem.at[z])

    def start(z, carry):
        load(z).start()
        return carry

    def patch(z, carry):
        load(z).wait()
        put_rows(cells, z, row_lo, row_hi, z)

        @pl.when(z == 0)
        def _():
            cells[:, 0] = own_lo[...]

        @pl.when(z == nz - 1)
        def _():
            cells[:, nz - 1] = own_hi[...]

        store(z).start()
        return carry

    def done(z, carry):
        store(z).wait()
        return carry

    lax.fori_loop(0, nz, start, 0)
    lax.fori_loop(0, nz, patch, 0)
    gather_tiles(cells, 0, blocks, normals, rows, rows_in)
    labels = lax.broadcasted_iota(jnp.int32, (table.shape[0], rows.shape[0]), 0)
    onehot = (labels == sections[...]).astype(jnp.float32)
    table[...] = jnp.dot(onehot, rows[...], precision=lax.Precision.HIGHEST, preferred_element_type=jnp.float32)
    lax.fori_loop(0, nz, done, 0)


def finish(field, own, rows, blocks, normals, sections, rows_in, total):
    nz = field.shape[1]
    tiles = blocks.shape[0]
    scratch = [VMEM(field.shape, jnp.float32), VMEM((tiles, LANES), jnp.float32)] + [pltpu.SemaphoreType.DMA((nz,))] * 2
    return call(finish_kernel, "finish", [f32(*field.shape), f32(total, LANES)],
                [ANYWHERE] + [IN_VMEM] * 4 + [IN_SMEM] * 2 + [IN_VMEM] * 2, [ANYWHERE, IN_VMEM], scratch, 24)(
        field, *own, *rows, blocks, normals, sections, rows_in)


def shift_along(block, axis, distance):
    count = lax.axis_size(axis)
    route = [(i, i + distance) for i in range(count) if 0 <= i + distance < count]
    return lax.ppermute(block, axis, route)


def swap(faces, axis):
    lo, hi = faces
    return [shift_along(hi, axis, 1), shift_along(lo, axis, -1)]


def local(adjoint_start, base_flow, wall_blocks, tile_sections, tile_normals, modes):
    z_lo, z_hi, y_lo, y_hi = pack(adjoint_start, base_flow)
    base_planes, base_rows = [z_lo, z_hi], [y_lo, y_hi]
    own, own_rows = base_planes, base_rows
    far = far_base = swap(base_planes, "span")
    far_rows = far_base_rows = swap(base_rows, "cross")
    field, rows_sum = adjoint_start, ()
    old, got = (), ()
    for step in range(STEPS):
        if step == 0:
            field, *edge = stencil(step, field, base_flow)
        else:
            field, *edge, rows_sum = stencil(step, field, base_flow, own, own_rows, wall_blocks, tile_normals, rows_sum)
            rows_sum = (rows_sum,)
        planes, rows = edge[:2], edge[2:]
        *planes, row_lo, row_hi = row_fix(planes, rows, own_rows, base_rows, far_rows, far_base_rows)
        coming = swap(planes, "span") if step < STEPS - 1 else ()
        out = plane_fix(planes, (row_lo, row_hi), own, base_planes, far_base, far, old, got)
        old, own, own_rows, got = own, out[:2], out[2:4], coming
        if step > 0:
            far = out[4:]
        if step < STEPS - 1:
            far_rows = swap(own_rows, "cross")
    sections = tile_sections.reshape(1, -1)
    crosses, spans = lax.axis_size("cross"), lax.axis_size("span")
    field, table = finish(field, own, own_rows, wall_blocks, tile_normals, sections, rows_sum[0], spans * crosses * SEC_DEV)
    parts = lax.all_to_all(table.reshape(spans * crosses, SEC_DEV, LANES), ("span", "cross"), 0, 0, tiled=True)
    section_sum = jnp.sum(parts, axis=0)
    modal_load = jnp.dot(section_sum, modes, precision=lax.Precision.HIGHEST, preferred_element_type=jnp.float32)
    return field, modal_load


def solution(mesh):
    placed = (
        P(None, "span", "cross", None),
        P(None, "span", "cross", None),
        P(("span", "cross")),
        P(("span", "cross"), None),
        P(None, ("span", "cross")),
        P(),
    )
    return jax.shard_map(
        local,
        mesh=mesh,
        in_specs=placed,
        out_specs=(P(None, "span", "cross", None), P(("span", "cross"), None)),
        check_vma=False,
    )
```

```python
import functools

import jax
import jax.numpy as jnp
from jax import lax
from jax.experimental import pallas as pl
from jax.experimental.pallas import tpu as pltpu
from jax.sharding import PartitionSpec as P

STEPS = 3
SEC_DEV = 2
TIME_STEP = 0.25
VISCOSITY = 0.1
LANES = 128
ROWS = 8
HALF = 0.5 * TIME_STEP
DIFF = TIME_STEP * VISCOSITY
KEEP = 1.0 - 6.0 * DIFF

VMEM = pltpu.VMEM
SMEM = pltpu.SMEM


def plane(field, f_lo, f_hi, slopes, base, put, ny, nx, put_slopes=None):
    lane = lax.broadcasted_iota(jnp.int32, (ROWS, LANES), 1)
    sub = lax.broadcasted_iota(jnp.int32, (ROWS, LANES), 0)
    last = nx // LANES - 1
    tiles = range(ny // ROWS)

    class Shifted:
        def __init__(self, get, c):
            self.get, self.c, self.kept = get, c, {}

        def once(self, key, make):
            if key not in self.kept:
                self.kept[key] = make()
            return self.kept[key]

        def tile(self, yt, k):
            return self.once((0, yt, k), lambda: self.get(self.c, yt, k))

        def left(self, yt, k):
            return self.once((1, yt, k), lambda: pltpu.roll(self.tile(yt, k), LANES - 1, 1))

        def right(self, yt, k):
            return self.once((2, yt, k), lambda: pltpu.roll(self.tile(yt, k), 1, 1))

        def up(self, yt, k):
            return self.once((3, yt, k), lambda: pltpu.roll(self.tile(yt, k), ROWS - 1, 0))

        def down(self, yt, k):
            return self.once((4, yt, k), lambda: pltpu.roll(self.tile(yt, k), 1, 0))

        def along_x(self, yt, k):
            return (jnp.where(lane == LANES - 1, self.left(yt, k + 1) if k < last else 0.0, self.left(yt, k)),
                    jnp.where(lane == 0, self.right(yt, k - 1) if k > 0 else 0.0, self.right(yt, k)))

        def along_y(self, yt, k):
            return (jnp.where(sub == ROWS - 1, self.up(yt + 1, k) if yt + 1 in tiles else 0.0, self.up(yt, k)),
                    jnp.where(sub == 0, self.down(yt - 1, k) if yt > 0 else 0.0, self.down(yt, k)))

    fields = [Shifted(field, c) for c in range(4)]
    flows = [Shifted(base, c) for c in range(3)]
    for k in range(nx // LANES):
        for yt in tiles:
            f = [fields[c].tile(yt, k) for c in range(4)]
            u = [flows[c].tile(yt, k) for c in range(3)]
            fs = [(fields[c].along_x(yt, k), fields[c].along_y(yt, k), (f_hi(c, yt, k), f_lo(c, yt, k))) for c in range(4)]
            slope = slopes(flows, yt, k)
            scaled = [HALF * u[d] for d in range(3)]
            up = [scaled[d] + DIFF for d in range(3)]
            down = [DIFF - scaled[d] for d in range(3)]
            out = []
            for i in range(3):
                acc = KEEP * f[i]
                for d in range(3):
                    acc = acc + up[d] * fs[i][d][0] + down[d] * fs[i][d][1]
                pull = fs[3][i][0] - fs[3][i][1]
                for j in range(3):
                    pull = pull + slope[i][j] * f[j]
                out.append(acc - HALF * pull)
            div = fs[0][0][0] - fs[0][0][1]
            for d in (1, 2):
                div = div + (fs[d][d][0] - fs[d][d][1])
            out.append(f[3] - HALF * div)
            for c in range(4):
                put(c, yt, k, out[c])
            if put_slopes is not None:
                put_slopes(yt, k, slope)


def fix(sign, d, f, u, beyond_f, beyond_u):
    half = sign * HALF
    coef = DIFF + half * u[d]
    out = [coef * beyond_f[i] for i in range(3)]
    pull = beyond_f[3]
    for j in range(3):
        pull = pull + beyond_u[j] * f[j]
    out[d] = out[d] - half * pull
    return out + [-half * beyond_f[d]]


def is_even(axis):
    return lax.axis_index(axis) % 2 == 0


def upper_sides(axis):
    even = is_even(axis)
    return even, jnp.logical_not(even)


def sign_of(upper):
    return jnp.where(upper, 1.0, -1.0).astype(jnp.float32)


def plane_tile(ref, c, yt, k):
    col = pl.ds(k * LANES, LANES)
    if ref.shape[1] == ROWS:
        return ref[2 * c + yt, :, col]
    return ref[c, pl.ds(yt * ROWS, ROWS), col]


def tile_of(ref, index):
    def get(c, yt, k):
        return ref[(c, *index, pl.ds(yt * ROWS, ROWS), pl.ds(k * LANES, LANES))]
    return get


def sides_kernel(field, base, z_even, z_odd, y_even, y_odd, f_all, b_all, sems):
    nz, ny, nx = field.shape[1:]
    even_y, even_z = is_even("cross"), is_even("span")

    def copies(z):
        return (pltpu.make_async_copy(field.at[:, z], f_all.at[:, z], sems.at[0, z]),
                pltpu.make_async_copy(base.at[:, z], b_all.at[:, z], sems.at[1, z]))

    def start(z, carry):
        for one in copies(z):
            one.start()
        return carry

    def rows(z, carry):
        for one in copies(z):
            one.wait()
        for src, off, n in ((f_all, 0, 4), (b_all, 4, 3)):
            for c in range(n):
                for k in range(nx // LANES):
                    col = pl.ds(k * LANES, LANES)
                    lo, hi = src[c, z, pl.ds(0, 1), col], src[c, z, pl.ds(ny - 1, 1), col]
                    y_even[c + off, z, pl.ds(k, 1), :] = jnp.where(even_y, hi, lo)
                    y_odd[c + off, z, pl.ds(k, 1), :] = jnp.where(even_y, lo, hi)
        return carry

    lax.fori_loop(0, nz, start, 0)
    lax.fori_loop(0, nz, rows, 0)
    z_up = jnp.where(even_z, nz - 1, 0)
    for out, z in ((z_even, z_up), (z_odd, nz - 1 - z_up)):
        out[0:4] = f_all[:, z]
        out[4:7] = b_all[:, z]


def f32(*shape):
    return jax.ShapeDtypeStruct(shape, jnp.float32)


def call(kernel, name, out_shape, in_specs, out_specs, scratch=(), mib=6, cost=None, aliases=None):
    return pl.pallas_call(
        kernel,
        out_shape=out_shape,
        in_specs=in_specs,
        out_specs=out_specs,
        scratch_shapes=list(scratch),
        compiler_params=pltpu.CompilerParams(vmem_limit_bytes=mib * 2**20),
        cost_estimate=cost,
        input_output_aliases=aliases or {},
        name=name,
    )


IN_VMEM = pl.BlockSpec(memory_space=VMEM)
IN_SMEM = pl.BlockSpec(memory_space=SMEM)
ANYWHERE = pl.BlockSpec(memory_space=pl.ANY)
FREE = pl.CostEstimate(flops=0, bytes_accessed=0, transcendentals=0)
IN_HBM = pl.BlockSpec(memory_space=pltpu.HBM)


def outer_sides(field, base):
    _, nz, ny, nx = field.shape
    outs = [f32(7, ny, nx)] * 2 + [f32(7, nz, nx // LANES, LANES)] * 2
    scratch = [VMEM(field.shape, jnp.float32), VMEM(base.shape, jnp.float32), pltpu.SemaphoreType.DMA((2, nz))]
    return call(sides_kernel, "outer_sides", outs, [ANYWHERE] * 2, [IN_VMEM] * 4, scratch, mib=52)(field, base)


def gather_tiles(cells, blocks, normals, rows):
    ny, nx = cells[0].shape[2:]
    per_row = nx // LANES
    row_bits, y_bits = per_row.bit_length() - 1, ny.bit_length() - 1
    sub = lax.broadcasted_iota(jnp.int32, (ROWS, LANES), 0)

    def gather(group, carry):
        kept = jnp.zeros((ROWS, LANES), jnp.float32)
        for j in range(ROWS):
            t = group * ROWS + j
            b = blocks[t]
            z = lax.shift_right_logical(b, row_bits + y_bits)
            y = lax.shift_right_logical(b, row_bits) & (ny - 1)
            near = pl.ds(pl.multiple_of(y & (ny - ROWS), ROWS), ROWS)
            col = pl.ds(pl.multiple_of((b & (per_row - 1)) * LANES, LANES), LANES)
            total = 0.0
            for c in range(4):
                run = cells[0][c, z, near, col]
                for more in cells[1:]:
                    run = run + more[c, z, near, col]
                total = total + normals[c, t] * run
            total = pltpu.roll(total, (j + ROWS - (y & (ROWS - 1))) & (ROWS - 1), 0)
            kept = jnp.where(sub == j, total, kept)
        rows[pl.ds(pl.multiple_of(group * ROWS, ROWS), ROWS), :] = TIME_STEP * kept
        return carry

    lax.fori_loop(0, rows.shape[0] // ROWS, gather, 0)


def put_rows(cells, even, rows_even, rows_odd, z, at):
    ny, nx = cells.shape[-2:]
    for c in range(4):
        for k in range(nx // LANES):
            col = pl.ds(k * LANES, LANES)
            one, two = rows_even[c, z, pl.ds(k, 1), :], rows_odd[c, z, pl.ds(k, 1), :]
            cells[(c, *at, pl.ds(0, 1), col)] = jnp.where(even, two, one)
            cells[(c, *at, pl.ds(ny - 1, 1), col)] = jnp.where(even, one, two)


def stencil_kernel(step, *refs):
    if step == 0:
        field, base, new, p_lo, p_hi, r_lo, r_hi, slope_ref = refs
    elif step < STEPS - 1:
        field, base, slope_ref, new, p_lo, p_hi, r_lo, r_hi = refs
    else:
        field, base, slope_ref, before, new, p_lo, p_hi, r_lo, r_hi, both = refs
    nz, ny, nx = field.shape[1:]

    def outside(c, yt, k):
        return jnp.zeros((ROWS, LANES), jnp.float32)

    def do(z, lower, upper):
        def at(yt, k):
            return (z, pl.ds(yt * ROWS, ROWS), pl.ds(k * LANES, LANES))

        def beside(ref, there, off):
            return tile_of(ref, (z + off,)) if there else outside

        def put(c, yt, k, value):
            new[(c, *at(yt, k))] = value
            if yt == 0:
                r_lo[c, z, pl.ds(k, 1), :] = value[:1]
            if yt == ny // ROWS - 1:
                r_hi[c, z, pl.ds(k, 1), :] = value[ROWS - 1:]
            if step == STEPS - 1:
                both[(c, *at(yt, k))] = before[(c, *at(yt, k))] + field[(c, *at(yt, k))]

        b_lo, b_hi = beside(base, lower, -1), beside(base, upper, 1)

        def slopes(flows, yt, k):
            if step > 0:
                return [[slope_ref[(3 * i + j, *at(yt, k))] for j in range(3)] for i in range(3)]
            found = []
            for along in (lambda j: flows[j].along_x(yt, k), lambda j: flows[j].along_y(yt, k), lambda j: (b_hi(j, yt, k), b_lo(j, yt, k))):
                sides = [along(j) for j in range(3)]
                found.append([hi - lo for hi, lo in sides])
            return found

        def put_slopes(yt, k, slope):
            for i in range(3):
                for j in range(3):
                    slope_ref[(3 * i + j, *at(yt, k))] = slope[i][j]

        plane(tile_of(field, (z,)), beside(field, lower, -1), beside(field, upper, 1), slopes, tile_of(base, (z,)), put, ny, nx,
              put_slopes if step == 0 else None)

    def body(z, carry):
        do(z, True, True)
        return carry

    do(0, False, True)
    p_lo[...] = new[:, 0]
    lax.fori_loop(1, nz - 1, body, 0)
    do(nz - 1, True, False)
    p_hi[...] = new[:, nz - 1]


def stencil(step, field, base, slopes=None, before=None):
    _, nz, ny, nx = field.shape
    outs = [f32(*field.shape)] + [f32(4, ny, nx)] * 2 + [f32(4, nz, nx // LANES, LANES)] * 2
    args = [field, base]
    if step == 0:
        outs.append(f32(9, nz, ny, nx))
    else:
        args.append(slopes)
    if step == STEPS - 1:
        args.append(before)
        outs.append(f32(*field.shape))
    ins = [IN_VMEM] * len(args)
    return call(functools.partial(stencil_kernel, step), "stencil", outs, ins, [IN_VMEM] * len(outs), cost=FREE)(*args)


def row_fix_kernel(after, p_lo, p_hi, r_lo, r_hi, own_e, own_o, base_e, base_o, far_e, far_o, fbase_e, fbase_o,
                   q_e, q_o, s_e, s_o):
    del after
    nz = r_lo.shape[1]
    uppers = upper_sides("cross")

    def body(z, carry):
        for upper, own, base, far, fbase, s in ((uppers[0], own_e, base_e, far_e, fbase_e, s_e),
                                                (uppers[1], own_o, base_o, far_o, fbase_o, s_o)):
            add = fix(sign_of(upper), 1, [own[c, z] for c in range(3)], [base[4 + c, z] for c in range(3)],
                      [far[c, z] for c in range(4)], [fbase[4 + c, z] for c in range(3)])
            for c in range(4):
                s[c, z] = jnp.where(upper, r_hi[c, z], r_lo[c, z]) + add[c]
        return carry

    lax.fori_loop(0, nz, body, 0)
    for upper, q in zip(upper_sides("span"), (q_e, q_o)):
        for c in range(4):
            q[c] = jnp.where(upper, p_hi[c], p_lo[c])
        put_rows(q, uppers[0], s_e, s_o, jnp.where(upper, nz - 1, 0), ())


def row_fix(after, planes, rows, own_rows, base_rows, far_rows, far_base_rows):
    outs = [f32(*planes[0].shape)] * 2 + [f32(*rows[0].shape)] * 2
    cost = FREE
    return call(row_fix_kernel, "row_fix", outs, [ANYWHERE] + [IN_VMEM] * 12, [IN_VMEM] * 4, cost=cost)(
        after, *planes, *rows, *own_rows, *base_rows, *far_rows, *far_base_rows)


def far_fix_kernel(got_e, got_o, far_e, far_o, fbase_e, fbase_o, old_e, old_o, base_e, base_o, next_e, next_o):
    _, ny, nx = got_e.shape
    span, ends = lax.axis_index("span"), lax.axis_size("span") - 1
    uppers = upper_sides("span")
    sides = (
        (uppers[0], got_e, far_e, fbase_e, old_e, base_e, next_e),
        (uppers[1], got_o, far_o, fbase_o, old_o, base_o, next_o),
    )
    for upper, got, far, fbase, old, base, nxt in sides:
        there = span != jnp.where(upper, ends, 0)
        for yt in range(ny // ROWS):
            for k in range(nx // LANES):
                tile = (pl.ds(yt * ROWS, ROWS), pl.ds(k * LANES, LANES))
                back = fix(-sign_of(upper), 2, [far[(c, *tile)] for c in range(3)], [fbase[(4 + c, *tile)] for c in range(3)],
                           [old[(c, *tile)] for c in range(4)], [base[(4 + c, *tile)] for c in range(3)])
                for c in range(4):
                    nxt[(c, *tile)] = jnp.where(there, got[(c, *tile)] + back[c], 0.0)


def far_fix(got, far, far_base, old, base):
    args = [*got, *far, *far_base, *old, *base]
    return call(far_fix_kernel, "far_fix", [f32(*got[0].shape)] * 2, [IN_VMEM] * len(args), [IN_VMEM] * 2, cost=FREE)(*args)


def plane_fix_kernel(big, q_e, q_o, s_e, s_o, own_e, own_o, base_e, base_o, fbase_e, fbase_o, far_e, far_o,
                     whole, out_e, out_o, row_e, row_o):
    del big
    _, ny, nx = q_e.shape
    nz = s_e.shape[1]
    even_y = is_even("cross")
    uppers = upper_sides("span")
    sides = (
        (uppers[0], q_e, own_e, base_e, fbase_e, far_e, out_e),
        (uppers[1], q_o, own_o, base_o, fbase_o, far_o, out_o),
    )
    row_e[...] = s_e[...]
    row_o[...] = s_o[...]
    for upper, q, own, base, fbase, far, out in sides:
        for yt in range(ny // ROWS):
            for k in range(nx // LANES):
                tile = (pl.ds(yt * ROWS, ROWS), pl.ds(k * LANES, LANES))
                add = fix(sign_of(upper), 2, [own[(c, *tile)] for c in range(3)], [base[(4 + c, *tile)] for c in range(3)],
                          [far[(c, *tile)] for c in range(4)], [fbase[(4 + c, *tile)] for c in range(3)])
                for c in range(4):
                    out[(c, *tile)] = q[(c, *tile)] + add[c]
        z = jnp.where(upper, nz - 1, 0)
        whole[:, z] = out[...]
        for c in range(4):
            for k in range(nx // LANES):
                col = pl.ds(k * LANES, LANES)
                lo, hi = out[c, pl.ds(0, 1), col], out[c, pl.ds(ny - 1, 1), col]
                row_e[c, z, pl.ds(k, 1), :] = jnp.where(even_y, hi, lo)
                row_o[c, z, pl.ds(k, 1), :] = jnp.where(even_y, lo, hi)

    def body(z, carry):
        put_rows(whole, even_y, s_e, s_o, z, (z,))
        return carry

    lax.fori_loop(1, nz - 1, body, 0)


def plane_fix(last, field, planes, rows, own, base, far_base, far):
    outs = [f32(*planes[0].shape)] * 2 + [f32(*rows[0].shape)] * 2
    scratch = []
    if last:
        outs, scratch = [], [VMEM(o.shape, o.dtype) for o in outs]
    outs = [f32(*field.shape)] + outs
    args = [field, *planes, *rows, *own, *base, *far_base, *far]
    return call(plane_fix_kernel, "plane_fix", outs, [IN_VMEM] * len(args), [IN_VMEM] * len(outs), scratch,
                cost=FREE, aliases={0: 0})(*args)


def finish_kernel(field, both, blocks, normals, sections, new, table, rows, sem):
    out = pltpu.make_async_copy(field, new, sem)
    out.start()
    gather_tiles((both, field), blocks, normals, rows)
    labels = lax.broadcasted_iota(jnp.int32, (table.shape[0], rows.shape[0]), 0)
    onehot = (labels == sections[...]).astype(jnp.float32)
    table[...] = jnp.dot(onehot, rows[...], precision=lax.Precision.HIGHEST, preferred_element_type=jnp.float32)
    out.wait()


def finish(field, both, blocks, normals, sections, total):
    scratch = [VMEM((blocks.shape[0], LANES), jnp.float32), pltpu.SemaphoreType.DMA]
    return call(finish_kernel, "finish", [f32(*field.shape), f32(total, LANES)],
                [IN_VMEM] * 2 + [IN_SMEM] * 2 + [IN_VMEM], [ANYWHERE, IN_VMEM], scratch)(
        field, both, blocks, normals, sections)


def swap(sides, axis):
    even, odd = sides
    count = lax.axis_size(axis)
    return [lax.ppermute(even, axis, [(i, i ^ 1) for i in range(count)]),
            lax.ppermute(odd, axis, [(i, ((i + 1) ^ 1) - 1) for i in range(1, count - 1)])]


def local(adjoint_start, base_flow, wall_blocks, tile_sections, tile_normals, modes):
    sides = outer_sides(adjoint_start, base_flow)
    own = base_planes = sides[:2]
    own_rows = base_rows = sides[2:]
    far_rows = far_base_rows = swap(base_rows, "cross")
    far = far_base = swap(base_planes, "span")
    field, before, slopes, both = adjoint_start, None, None, None
    old, got, after = None, None, base_planes[0]
    for step in range(STEPS):
        fresh, *edge = stencil(step, field, base_flow, slopes, before)
        if step == 0:
            slopes = edge.pop()
        else:
            far = far_fix(got, far, far_base, old, base_planes)
            after = far[0]
            if step == STEPS - 1:
                both = edge.pop()
        *planes, row_lo, row_hi = row_fix(after, edge[:2], edge[2:], own_rows, base_rows, far_rows, far_base_rows)
        if step < STEPS - 1:
            got = swap(planes, "span")
        before, old = field, own
        field, *out = plane_fix(step == STEPS - 1, fresh, planes, (row_lo, row_hi), own, base_planes, far_base, far)
        own, own_rows = out[:2], out[2:]
        if step < STEPS - 1:
            far_rows = swap(own_rows, "cross")
    sections = tile_sections.reshape(1, -1)
    devices = lax.axis_size("cross") * lax.axis_size("span")
    field, table = finish(field, both, wall_blocks, tile_normals, sections, devices * SEC_DEV)
    parts = lax.all_to_all(table.reshape(devices, SEC_DEV, LANES), ("span", "cross"), 0, 0, tiled=True)
    section_sum = jnp.sum(parts, axis=0)
    modal_load = jnp.dot(section_sum, modes, precision=lax.Precision.HIGHEST, preferred_element_type=jnp.float32)
    return field, modal_load


def solution(mesh):
    placed = (
        P(None, "span", "cross", None),
        P(None, "span", "cross", None),
        P(("span", "cross")),
        P(("span", "cross"), None),
        P(None, ("span", "cross")),
        P(),
    )
    return jax.shard_map(
        local,
        mesh=mesh,
        in_specs=placed,
        out_specs=(P(None, "span", "cross", None), P(("span", "cross"), None)),
        check_vma=False,
    )
```

```python
import functools

import jax
import jax.numpy as jnp
from jax import lax
from jax.experimental import pallas as pl
from jax.experimental.pallas import tpu as pltpu
from jax.sharding import PartitionSpec as P

STEPS = 3
SEC_DEV = 2
TIME_STEP = 0.25
VISCOSITY = 0.1
LANES = 128
ROWS = 8
HALF = 0.5 * TIME_STEP
DIFF = TIME_STEP * VISCOSITY
KEEP = 1.0 - 6.0 * DIFF

VMEM = pltpu.VMEM
SMEM = pltpu.SMEM


def plane(field, f_lo, f_hi, slopes, base, put, ny, nx, put_slopes=None):
    lane = lax.broadcasted_iota(jnp.int32, (ROWS, LANES), 1)
    sub = lax.broadcasted_iota(jnp.int32, (ROWS, LANES), 0)
    last = nx // LANES - 1
    tiles = range(ny // ROWS)

    class Shifted:
        def __init__(self, get, c):
            self.get, self.c, self.kept = get, c, {}

        def once(self, key, make):
            if key not in self.kept:
                self.kept[key] = make()
            return self.kept[key]

        def tile(self, yt, k):
            return self.once((0, yt, k), lambda: self.get(self.c, yt, k))

        def left(self, yt, k):
            return self.once((1, yt, k), lambda: pltpu.roll(self.tile(yt, k), LANES - 1, 1))

        def right(self, yt, k):
            return self.once((2, yt, k), lambda: pltpu.roll(self.tile(yt, k), 1, 1))

        def up(self, yt, k):
            return self.once((3, yt, k), lambda: pltpu.roll(self.tile(yt, k), ROWS - 1, 0))

        def down(self, yt, k):
            return self.once((4, yt, k), lambda: pltpu.roll(self.tile(yt, k), 1, 0))

        def along_x(self, yt, k):
            return (jnp.where(lane == LANES - 1, self.left(yt, k + 1) if k < last else 0.0, self.left(yt, k)),
                    jnp.where(lane == 0, self.right(yt, k - 1) if k > 0 else 0.0, self.right(yt, k)))

        def along_y(self, yt, k):
            return (jnp.where(sub == ROWS - 1, self.up(yt + 1, k) if yt + 1 in tiles else 0.0, self.up(yt, k)),
                    jnp.where(sub == 0, self.down(yt - 1, k) if yt > 0 else 0.0, self.down(yt, k)))

    fields = [Shifted(field, c) for c in range(4)]
    flows = [Shifted(base, c) for c in range(3)]
    for k in range(nx // LANES):
        for yt in tiles:
            f = [fields[c].tile(yt, k) for c in range(4)]
            u = [flows[c].tile(yt, k) for c in range(3)]
            fs = [(fields[c].along_x(yt, k), fields[c].along_y(yt, k), (f_hi(c, yt, k), f_lo(c, yt, k))) for c in range(4)]
            slope = slopes(flows, yt, k)
            scaled = [HALF * u[d] for d in range(3)]
            up = [scaled[d] + DIFF for d in range(3)]
            down = [DIFF - scaled[d] for d in range(3)]
            out = []
            for i in range(3):
                acc = KEEP * f[i]
                for d in range(3):
                    acc = acc + up[d] * fs[i][d][0] + down[d] * fs[i][d][1]
                pull = fs[3][i][0] - fs[3][i][1]
                for j in range(3):
                    pull = pull + slope[i][j] * f[j]
                out.append(acc - HALF * pull)
            div = fs[0][0][0] - fs[0][0][1]
            for d in (1, 2):
                div = div + (fs[d][d][0] - fs[d][d][1])
            out.append(f[3] - HALF * div)
            for c in range(4):
                put(c, yt, k, out[c])
            if put_slopes is not None:
                put_slopes(yt, k, slope)


def fix(sign, d, f, u, beyond_f, beyond_u):
    half = sign * HALF
    coef = DIFF + half * u[d]
    out = [coef * beyond_f[i] for i in range(3)]
    pull = beyond_f[3]
    for j in range(3):
        pull = pull + beyond_u[j] * f[j]
    out[d] = out[d] - half * pull
    return out + [-half * beyond_f[d]]


def is_even(axis):
    return lax.axis_index(axis) % 2 == 0


def upper_sides(axis):
    even = is_even(axis)
    return even, jnp.logical_not(even)


def sign_of(upper):
    return jnp.where(upper, 1.0, -1.0).astype(jnp.float32)


def plane_tile(ref, c, yt, k):
    col = pl.ds(k * LANES, LANES)
    if ref.shape[1] == ROWS:
        return ref[2 * c + yt, :, col]
    return ref[c, pl.ds(yt * ROWS, ROWS), col]


def tile_of(ref, index):
    def get(c, yt, k):
        return ref[(c, *index, pl.ds(yt * ROWS, ROWS), pl.ds(k * LANES, LANES))]
    return get


def sides_kernel(field, base, z_even, z_odd, y_even, y_odd, f_all, b_all, sems):
    nz, ny, nx = field.shape[1:]
    even_y, even_z = is_even("cross"), is_even("span")

    def copies(z):
        return (pltpu.make_async_copy(field.at[:, z], f_all.at[:, z], sems.at[0, z]),
                pltpu.make_async_copy(base.at[:, z], b_all.at[:, z], sems.at[1, z]))

    def start(z, carry):
        for one in copies(z):
            one.start()
        return carry

    def rows(z, carry):
        for one in copies(z):
            one.wait()
        for src, off, n in ((f_all, 0, 4), (b_all, 4, 3)):
            for c in range(n):
                for k in range(nx // LANES):
                    col = pl.ds(k * LANES, LANES)
                    lo, hi = src[c, z, pl.ds(0, 1), col], src[c, z, pl.ds(ny - 1, 1), col]
                    y_even[c + off, z, pl.ds(k, 1), :] = jnp.where(even_y, hi, lo)
                    y_odd[c + off, z, pl.ds(k, 1), :] = jnp.where(even_y, lo, hi)
        return carry

    lax.fori_loop(0, nz, start, 0)
    lax.fori_loop(0, nz, rows, 0)
    z_up = jnp.where(even_z, nz - 1, 0)
    for out, z in ((z_even, z_up), (z_odd, nz - 1 - z_up)):
        out[0:4] = f_all[:, z]
        out[4:7] = b_all[:, z]


def f32(*shape):
    return jax.ShapeDtypeStruct(shape, jnp.float32)


def call(kernel, name, out_shape, in_specs, out_specs, scratch=(), mib=6, cost=None, aliases=None):
    return pl.pallas_call(
        kernel,
        out_shape=out_shape,
        in_specs=in_specs,
        out_specs=out_specs,
        scratch_shapes=list(scratch),
        compiler_params=pltpu.CompilerParams(vmem_limit_bytes=mib * 2**20),
        cost_estimate=cost,
        input_output_aliases=aliases or {},
        name=name,
    )


IN_VMEM = pl.BlockSpec(memory_space=VMEM)
IN_SMEM = pl.BlockSpec(memory_space=SMEM)
ANYWHERE = pl.BlockSpec(memory_space=pl.ANY)
FREE = pl.CostEstimate(flops=0, bytes_accessed=0, transcendentals=0)
IN_HBM = pl.BlockSpec(memory_space=pltpu.HBM)


def outer_sides(field, base):
    _, nz, ny, nx = field.shape
    outs = [f32(7, ny, nx)] * 2 + [f32(7, nz, nx // LANES, LANES)] * 2
    scratch = [VMEM(field.shape, jnp.float32), VMEM(base.shape, jnp.float32), pltpu.SemaphoreType.DMA((2, nz))]
    return call(sides_kernel, "outer_sides", outs, [ANYWHERE] * 2, [IN_VMEM] * 4, scratch, mib=52)(field, base)


def gather_tiles(cells, blocks, weights, rows):
    ny, nx = cells[0].shape[2:]
    per_row = nx // LANES
    row_bits, y_bits = per_row.bit_length() - 1, ny.bit_length() - 1
    sub = lax.broadcasted_iota(jnp.int32, (ROWS, LANES), 0)

    def gather(group, carry):
        kept = jnp.zeros((ROWS, LANES), jnp.float32)
        for j in range(ROWS):
            t = group * ROWS + j
            b = blocks[t]
            z = lax.shift_right_logical(b, row_bits + y_bits)
            y = lax.shift_right_logical(b, row_bits) & (ny - 1)
            near = pl.ds(pl.multiple_of(y & (ny - ROWS), ROWS), ROWS)
            col = pl.ds(pl.multiple_of((b & (per_row - 1)) * LANES, LANES), LANES)
            total = 0.0
            for c in range(4):
                run = cells[0][c, z, near, col]
                for more in cells[1:]:
                    run = run + more[c, z, near, col]
                total = total + weights[c, group, pl.ds(j, 1), :] * run
            total = pltpu.roll(total, (j + ROWS - (y & (ROWS - 1))) & (ROWS - 1), 0)
            kept = jnp.where(sub == j, total, kept)
        rows[pl.ds(pl.multiple_of(group * ROWS, ROWS), ROWS), :] = TIME_STEP * kept
        return carry

    lax.fori_loop(0, rows.shape[0] // ROWS, gather, 0)


def put_rows(cells, even, rows_even, rows_odd, z, at):
    ny, nx = cells.shape[-2:]
    for c in range(4):
        for k in range(nx // LANES):
            col = pl.ds(k * LANES, LANES)
            one, two = rows_even[c, z, pl.ds(k, 1), :], rows_odd[c, z, pl.ds(k, 1), :]
            cells[(c, *at, pl.ds(0, 1), col)] = jnp.where(even, two, one)
            cells[(c, *at, pl.ds(ny - 1, 1), col)] = jnp.where(even, one, two)


def stencil_kernel(step, *refs):
    if step == 0:
        field, base, new, p_lo, p_hi, r_lo, r_hi, slope_ref = refs
    elif step < STEPS - 1:
        field, base, slope_ref, new, p_lo, p_hi, r_lo, r_hi = refs
    else:
        field, base, slope_ref, before, new, p_lo, p_hi, r_lo, r_hi, both = refs
    nz, ny, nx = field.shape[1:]

    def outside(c, yt, k):
        return jnp.zeros((ROWS, LANES), jnp.float32)

    def do(z, lower, upper):
        def at(yt, k):
            return (z, pl.ds(yt * ROWS, ROWS), pl.ds(k * LANES, LANES))

        def beside(ref, there, off):
            return tile_of(ref, (z + off,)) if there else outside

        def put(c, yt, k, value):
            new[(c, *at(yt, k))] = value
            if yt == 0:
                r_lo[c, z, pl.ds(k, 1), :] = value[:1]
            if yt == ny // ROWS - 1:
                r_hi[c, z, pl.ds(k, 1), :] = value[ROWS - 1:]
            if step == STEPS - 1:
                both[(c, *at(yt, k))] = before[(c, *at(yt, k))] + field[(c, *at(yt, k))]

        b_lo, b_hi = beside(base, lower, -1), beside(base, upper, 1)

        def slopes(flows, yt, k):
            if step > 0:
                return [[slope_ref[(3 * i + j, *at(yt, k))] for j in range(3)] for i in range(3)]
            found = []
            for along in (lambda j: flows[j].along_x(yt, k), lambda j: flows[j].along_y(yt, k), lambda j: (b_hi(j, yt, k), b_lo(j, yt, k))):
                sides = [along(j) for j in range(3)]
                found.append([hi - lo for hi, lo in sides])
            return found

        def put_slopes(yt, k, slope):
            for i in range(3):
                for j in range(3):
                    slope_ref[(3 * i + j, *at(yt, k))] = slope[i][j]

        plane(tile_of(field, (z,)), beside(field, lower, -1), beside(field, upper, 1), slopes, tile_of(base, (z,)), put, ny, nx,
              put_slopes if step == 0 else None)

    def body(z, carry):
        do(z, True, True)
        return carry

    do(0, False, True)
    p_lo[...] = new[:, 0]
    lax.fori_loop(1, nz - 1, body, 0)
    do(nz - 1, True, False)
    p_hi[...] = new[:, nz - 1]


def stencil(step, field, base, slopes=None, before=None):
    _, nz, ny, nx = field.shape
    outs = [f32(*field.shape)] + [f32(4, ny, nx)] * 2 + [f32(4, nz, nx // LANES, LANES)] * 2
    args = [field, base]
    if step == 0:
        outs.append(f32(9, nz, ny, nx))
    else:
        args.append(slopes)
    if step == STEPS - 1:
        args.append(before)
        outs.append(f32(*field.shape))
    ins = [IN_VMEM] * len(args)
    return call(functools.partial(stencil_kernel, step), "stencil", outs, ins, [IN_VMEM] * len(outs), cost=FREE)(*args)


def row_fix_kernel(after, p_lo, p_hi, r_lo, r_hi, own_e, own_o, base_e, base_o, far_e, far_o, fbase_e, fbase_o,
                   q_e, q_o, s_e, s_o):
    del after
    nz = r_lo.shape[1]
    uppers = upper_sides("cross")

    def body(z, carry):
        for upper, own, base, far, fbase, s in ((uppers[0], own_e, base_e, far_e, fbase_e, s_e),
                                                (uppers[1], own_o, base_o, far_o, fbase_o, s_o)):
            add = fix(sign_of(upper), 1, [own[c, z] for c in range(3)], [base[4 + c, z] for c in range(3)],
                      [far[c, z] for c in range(4)], [fbase[4 + c, z] for c in range(3)])
            for c in range(4):
                s[c, z] = jnp.where(upper, r_hi[c, z], r_lo[c, z]) + add[c]
        return carry

    lax.fori_loop(0, nz, body, 0)
    for upper, q in zip(upper_sides("span"), (q_e, q_o)):
        for c in range(4):
            q[c] = jnp.where(upper, p_hi[c], p_lo[c])
        put_rows(q, uppers[0], s_e, s_o, jnp.where(upper, nz - 1, 0), ())


def row_fix(after, planes, rows, own_rows, base_rows, far_rows, far_base_rows):
    outs = [f32(*planes[0].shape)] * 2 + [f32(*rows[0].shape)] * 2
    cost = FREE
    return call(row_fix_kernel, "row_fix", outs, [ANYWHERE] + [IN_VMEM] * 12, [IN_VMEM] * 4, cost=cost)(
        after, *planes, *rows, *own_rows, *base_rows, *far_rows, *far_base_rows)


def far_fix_kernel(got_e, got_o, far_e, far_o, fbase_e, fbase_o, old_e, old_o, base_e, base_o, next_e, next_o):
    _, ny, nx = got_e.shape
    span, ends = lax.axis_index("span"), lax.axis_size("span") - 1
    uppers = upper_sides("span")
    sides = (
        (uppers[0], got_e, far_e, fbase_e, old_e, base_e, next_e),
        (uppers[1], got_o, far_o, fbase_o, old_o, base_o, next_o),
    )
    for upper, got, far, fbase, old, base, nxt in sides:
        there = span != jnp.where(upper, ends, 0)
        for yt in range(ny // ROWS):
            for k in range(nx // LANES):
                tile = (pl.ds(yt * ROWS, ROWS), pl.ds(k * LANES, LANES))
                back = fix(-sign_of(upper), 2, [far[(c, *tile)] for c in range(3)], [fbase[(4 + c, *tile)] for c in range(3)],
                           [old[(c, *tile)] for c in range(4)], [base[(4 + c, *tile)] for c in range(3)])
                for c in range(4):
                    nxt[(c, *tile)] = jnp.where(there, got[(c, *tile)] + back[c], 0.0)


def far_fix(got, far, far_base, old, base):
    args = [*got, *far, *far_base, *old, *base]
    return call(far_fix_kernel, "far_fix", [f32(*got[0].shape)] * 2, [IN_VMEM] * len(args), [IN_VMEM] * 2, cost=FREE)(*args)


def plane_fix_kernel(big, q_e, q_o, s_e, s_o, own_e, own_o, base_e, base_o, fbase_e, fbase_o, far_e, far_o,
                     whole, out_e, out_o, row_e, row_o):
    del big
    _, ny, nx = q_e.shape
    nz = s_e.shape[1]
    even_y = is_even("cross")
    uppers = upper_sides("span")
    sides = (
        (uppers[0], q_e, own_e, base_e, fbase_e, far_e, out_e),
        (uppers[1], q_o, own_o, base_o, fbase_o, far_o, out_o),
    )
    row_e[...] = s_e[...]
    row_o[...] = s_o[...]
    for upper, q, own, base, fbase, far, out in sides:
        for yt in range(ny // ROWS):
            for k in range(nx // LANES):
                tile = (pl.ds(yt * ROWS, ROWS), pl.ds(k * LANES, LANES))
                add = fix(sign_of(upper), 2, [own[(c, *tile)] for c in range(3)], [base[(4 + c, *tile)] for c in range(3)],
                          [far[(c, *tile)] for c in range(4)], [fbase[(4 + c, *tile)] for c in range(3)])
                for c in range(4):
                    out[(c, *tile)] = q[(c, *tile)] + add[c]
        z = jnp.where(upper, nz - 1, 0)
        whole[:, z] = out[...]
        for c in range(4):
            for k in range(nx // LANES):
                col = pl.ds(k * LANES, LANES)
                lo, hi = out[c, pl.ds(0, 1), col], out[c, pl.ds(ny - 1, 1), col]
                row_e[c, z, pl.ds(k, 1), :] = jnp.where(even_y, hi, lo)
                row_o[c, z, pl.ds(k, 1), :] = jnp.where(even_y, lo, hi)

    def body(z, carry):
        put_rows(whole, even_y, s_e, s_o, z, (z,))
        return carry

    lax.fori_loop(1, nz - 1, body, 0)


def plane_fix(last, field, planes, rows, own, base, far_base, far):
    outs = [f32(*planes[0].shape)] * 2 + [f32(*rows[0].shape)] * 2
    scratch = []
    if last:
        outs, scratch = [], [VMEM(o.shape, o.dtype) for o in outs]
    outs = [f32(*field.shape)] + outs
    args = [field, *planes, *rows, *own, *base, *far_base, *far]
    return call(plane_fix_kernel, "plane_fix", outs, [IN_VMEM] * len(args), [IN_VMEM] * len(outs), scratch,
                cost=FREE, aliases={0: 0})(*args)


def spread_kernel(normals, weights):
    count = normals.shape[1]
    across = jnp.concatenate([normals[...], jnp.zeros((ROWS - 4, count), jnp.float32)]).T
    for c in range(4):
        weights[c] = jnp.broadcast_to(across[:, c:c + 1], (count, LANES)).reshape(count // ROWS, ROWS, LANES)


def spread(normals):
    return call(spread_kernel, "spread", f32(4, normals.shape[1] // ROWS, ROWS, LANES), [IN_VMEM], IN_VMEM, cost=FREE)(normals)


def finish_kernel(field, both, blocks, weights, sections, new, table, rows, sems):
    nz = field.shape[1]

    def out(z):
        return pltpu.make_async_copy(field.at[:, z], new.at[:, z], sems.at[z])

    for z in range(nz):
        out(z).start()
    gather_tiles((both, field), blocks, weights, rows)
    labels = lax.broadcasted_iota(jnp.int32, (table.shape[0], rows.shape[0]), 0)
    onehot = (labels == sections[...]).astype(jnp.float32).astype(jnp.bfloat16)
    left, parts = rows[...], []
    for _ in range(3):
        parts.append(left.astype(jnp.bfloat16))
        left = left - parts[-1].astype(jnp.float32)
    sums = jnp.dot(onehot, jnp.concatenate(parts, axis=1), preferred_element_type=jnp.float32)
    table[...] = sums[:, :LANES] + sums[:, LANES:2 * LANES] + sums[:, 2 * LANES:]
    for z in range(nz):
        out(z).wait()


def finish(field, both, blocks, weights, sections, total):
    scratch = [VMEM((blocks.shape[0], LANES), jnp.float32), pltpu.SemaphoreType.DMA((field.shape[1],))]
    return call(finish_kernel, "finish", [f32(*field.shape), f32(total, LANES)],
                [IN_VMEM] * 2 + [IN_SMEM] + [IN_VMEM] * 2, [ANYWHERE, IN_VMEM], scratch)(
        field, both, blocks, weights, sections)


def swap(sides, axis):
    even, odd = sides
    count = lax.axis_size(axis)
    return [lax.ppermute(even, axis, [(i, i ^ 1) for i in range(count)]),
            lax.ppermute(odd, axis, [(i, ((i + 1) ^ 1) - 1) for i in range(1, count - 1)])]


def local(adjoint_start, base_flow, wall_blocks, tile_sections, tile_normals, modes):
    sides = outer_sides(adjoint_start, base_flow)
    own = base_planes = sides[:2]
    own_rows = base_rows = sides[2:]
    far_rows = far_base_rows = swap(base_rows, "cross")
    far = far_base = swap(base_planes, "span")
    field, before, slopes, both = adjoint_start, None, None, None
    old, got, after = None, None, base_planes[0]
    for step in range(STEPS):
        fresh, *edge = stencil(step, field, base_flow, slopes, before)
        if step == 0:
            slopes = edge.pop()
        else:
            far = far_fix(got, far, far_base, old, base_planes)
            after = far[0]
            if step == STEPS - 1:
                both = edge.pop()
        *planes, row_lo, row_hi = row_fix(after, edge[:2], edge[2:], own_rows, base_rows, far_rows, far_base_rows)
        if step < STEPS - 1:
            got = swap(planes, "span")
        before, old = field, own
        field, *out = plane_fix(step == STEPS - 1, fresh, planes, (row_lo, row_hi), own, base_planes, far_base, far)
        own, own_rows = out[:2], out[2:]
        if step < STEPS - 1:
            far_rows = swap(own_rows, "cross")
    sections = tile_sections.reshape(1, -1)
    devices = lax.axis_size("cross") * lax.axis_size("span")
    field, table = finish(field, both, wall_blocks, spread(tile_normals), sections, devices * SEC_DEV)
    parts = lax.all_to_all(table.reshape(devices, SEC_DEV, LANES), ("span", "cross"), 0, 0, tiled=True)
    section_sum = jnp.sum(parts, axis=0)
    modal_load = jnp.dot(section_sum, modes, precision=lax.Precision.HIGHEST, preferred_element_type=jnp.float32)
    return field, modal_load


def solution(mesh):
    placed = (
        P(None, "span", "cross", None),
        P(None, "span", "cross", None),
        P(("span", "cross")),
        P(("span", "cross"), None),
        P(None, ("span", "cross")),
        P(),
    )
    return jax.shard_map(
        local,
        mesh=mesh,
        in_specs=placed,
        out_specs=(P(None, "span", "cross", None), P(("span", "cross"), None)),
        check_vma=False,
    )
```

```python
import functools

import jax
import jax.numpy as jnp
from jax import lax
from jax.experimental import pallas as pl
from jax.experimental.pallas import tpu as pltpu
from jax.sharding import PartitionSpec as P

STEPS = 3
SEC_DEV = 2
TIME_STEP = 0.25
VISCOSITY = 0.1
LANES = 128
ROWS = 8
HALF = 0.5 * TIME_STEP
DIFF = TIME_STEP * VISCOSITY
KEEP = 1.0 - 6.0 * DIFF

VMEM = pltpu.VMEM
SMEM = pltpu.SMEM


def plane(field, f_lo, f_hi, slopes, base, put, ny, nx, put_slopes=None):
    lane = lax.broadcasted_iota(jnp.int32, (ROWS, LANES), 1)
    sub = lax.broadcasted_iota(jnp.int32, (ROWS, LANES), 0)
    last = nx // LANES - 1
    tiles = range(ny // ROWS)

    class Shifted:
        def __init__(self, get, c):
            self.get, self.c, self.kept = get, c, {}

        def once(self, key, make):
            if key not in self.kept:
                self.kept[key] = make()
            return self.kept[key]

        def tile(self, yt, k):
            return self.once((0, yt, k), lambda: self.get(self.c, yt, k))

        def left(self, yt, k):
            return self.once((1, yt, k), lambda: pltpu.roll(self.tile(yt, k), LANES - 1, 1))

        def right(self, yt, k):
            return self.once((2, yt, k), lambda: pltpu.roll(self.tile(yt, k), 1, 1))

        def up(self, yt, k):
            return self.once((3, yt, k), lambda: pltpu.roll(self.tile(yt, k), ROWS - 1, 0))

        def down(self, yt, k):
            return self.once((4, yt, k), lambda: pltpu.roll(self.tile(yt, k), 1, 0))

        def along_x(self, yt, k):
            return (jnp.where(lane == LANES - 1, self.left(yt, k + 1) if k < last else 0.0, self.left(yt, k)),
                    jnp.where(lane == 0, self.right(yt, k - 1) if k > 0 else 0.0, self.right(yt, k)))

        def along_y(self, yt, k):
            return (jnp.where(sub == ROWS - 1, self.up(yt + 1, k) if yt + 1 in tiles else 0.0, self.up(yt, k)),
                    jnp.where(sub == 0, self.down(yt - 1, k) if yt > 0 else 0.0, self.down(yt, k)))

    fields = [Shifted(field, c) for c in range(4)]
    flows = [Shifted(base, c) for c in range(3)]
    for k in range(nx // LANES):
        for yt in tiles:
            f = [fields[c].tile(yt, k) for c in range(4)]
            u = [flows[c].tile(yt, k) for c in range(3)]
            fs = [(fields[c].along_x(yt, k), fields[c].along_y(yt, k), (f_hi(c, yt, k), f_lo(c, yt, k))) for c in range(4)]
            slope = slopes(flows, yt, k)
            scaled = [HALF * u[d] for d in range(3)]
            up = [scaled[d] + DIFF for d in range(3)]
            down = [DIFF - scaled[d] for d in range(3)]
            out = []
            for i in range(3):
                acc = KEEP * f[i]
                for d in range(3):
                    acc = acc + up[d] * fs[i][d][0] + down[d] * fs[i][d][1]
                pull = fs[3][i][0] - fs[3][i][1]
                for j in range(3):
                    pull = pull + slope[i][j] * f[j]
                out.append(acc - HALF * pull)
            div = fs[0][0][0] - fs[0][0][1]
            for d in (1, 2):
                div = div + (fs[d][d][0] - fs[d][d][1])
            out.append(f[3] - HALF * div)
            for c in range(4):
                put(c, yt, k, out[c])
            if put_slopes is not None:
                put_slopes(yt, k, slope)


def fix(sign, d, f, u, beyond_f, beyond_u):
    half = sign * HALF
    coef = DIFF + half * u[d]
    out = [coef * beyond_f[i] for i in range(3)]
    pull = beyond_f[3]
    for j in range(3):
        pull = pull + beyond_u[j] * f[j]
    out[d] = out[d] - half * pull
    return out + [-half * beyond_f[d]]


def is_even(axis):
    return lax.axis_index(axis) % 2 == 0


def upper_sides(axis):
    even = is_even(axis)
    return even, jnp.logical_not(even)


def sign_of(upper):
    return jnp.where(upper, 1.0, -1.0).astype(jnp.float32)


def plane_tile(ref, c, yt, k):
    col = pl.ds(k * LANES, LANES)
    if ref.shape[1] == ROWS:
        return ref[2 * c + yt, :, col]
    return ref[c, pl.ds(yt * ROWS, ROWS), col]


def tile_of(ref, index):
    def get(c, yt, k):
        return ref[(c, *index, pl.ds(yt * ROWS, ROWS), pl.ds(k * LANES, LANES))]
    return get


def sides_kernel(field, base, z_even, z_odd, y_even, y_odd, f_all, b_all, sems):
    nz, ny, nx = field.shape[1:]
    even_y, even_z = is_even("cross"), is_even("span")

    def copies(z):
        return (pltpu.make_async_copy(field.at[:, z], f_all.at[:, z], sems.at[0, z]),
                pltpu.make_async_copy(base.at[:, z], b_all.at[:, z], sems.at[1, z]))

    def start(z, carry):
        for one in copies(z):
            one.start()
        return carry

    def rows(z, carry):
        for one in copies(z):
            one.wait()
        for src, off, n in ((f_all, 0, 4), (b_all, 4, 3)):
            for c in range(n):
                for k in range(nx // LANES):
                    col = pl.ds(k * LANES, LANES)
                    lo, hi = src[c, z, pl.ds(0, 1), col], src[c, z, pl.ds(ny - 1, 1), col]
                    y_even[c + off, z, pl.ds(k, 1), :] = jnp.where(even_y, hi, lo)
                    y_odd[c + off, z, pl.ds(k, 1), :] = jnp.where(even_y, lo, hi)
        return carry

    lax.fori_loop(0, nz, start, 0)
    lax.fori_loop(0, nz, rows, 0)
    z_up = jnp.where(even_z, nz - 1, 0)
    for out, z in ((z_even, z_up), (z_odd, nz - 1 - z_up)):
        out[0:4] = f_all[:, z]
        out[4:7] = b_all[:, z]


def f32(*shape):
    return jax.ShapeDtypeStruct(shape, jnp.float32)


def call(kernel, name, out_shape, in_specs, out_specs, scratch=(), mib=6, cost=None, aliases=None):
    return pl.pallas_call(
        kernel,
        out_shape=out_shape,
        in_specs=in_specs,
        out_specs=out_specs,
        scratch_shapes=list(scratch),
        compiler_params=pltpu.CompilerParams(vmem_limit_bytes=mib * 2**20),
        cost_estimate=cost,
        input_output_aliases=aliases or {},
        name=name,
    )


IN_VMEM = pl.BlockSpec(memory_space=VMEM)
IN_SMEM = pl.BlockSpec(memory_space=SMEM)
ANYWHERE = pl.BlockSpec(memory_space=pl.ANY)
FREE = pl.CostEstimate(flops=0, bytes_accessed=0, transcendentals=0)
IN_HBM = pl.BlockSpec(memory_space=pltpu.HBM)


def outer_sides(field, base):
    _, nz, ny, nx = field.shape
    outs = [f32(7, ny, nx)] * 2 + [f32(7, nz, nx // LANES, LANES)] * 2
    scratch = [VMEM(field.shape, jnp.float32), VMEM(base.shape, jnp.float32), pltpu.SemaphoreType.DMA((2, nz))]
    return call(sides_kernel, "outer_sides", outs, [ANYWHERE] * 2, [IN_VMEM] * 4, scratch, mib=52)(field, base)


def gather_tiles(cells, blocks, weights, rows):
    ny, nx = cells[0].shape[2:]
    per_row = nx // LANES
    row_bits, y_bits = per_row.bit_length() - 1, ny.bit_length() - 1
    sub = lax.broadcasted_iota(jnp.int32, (ROWS, LANES), 0)

    def gather(group, carry):
        kept = jnp.zeros((ROWS, LANES), jnp.float32)
        for j in range(ROWS):
            t = group * ROWS + j
            b = blocks[t]
            z = lax.shift_right_logical(b, row_bits + y_bits)
            y = lax.shift_right_logical(b, row_bits) & (ny - 1)
            near = pl.ds(pl.multiple_of(y & (ny - ROWS), ROWS), ROWS)
            col = pl.ds(pl.multiple_of((b & (per_row - 1)) * LANES, LANES), LANES)
            total = 0.0
            for c in range(4):
                run = cells[0][c, z, near, col]
                for more in cells[1:]:
                    run = run + more[c, z, near, col]
                total = total + weights[c, group, pl.ds(j, 1), :] * run
            total = pltpu.roll(total, (j + ROWS - (y & (ROWS - 1))) & (ROWS - 1), 0)
            kept = jnp.where(sub == j, total, kept)
        rows[pl.ds(pl.multiple_of(group * ROWS, ROWS), ROWS), :] = TIME_STEP * kept
        return carry

    lax.fori_loop(0, rows.shape[0] // ROWS, gather, 0)


def put_rows(cells, even, rows_even, rows_odd, z, at):
    ny, nx = cells.shape[-2:]
    for c in range(4):
        for k in range(nx // LANES):
            col = pl.ds(k * LANES, LANES)
            one, two = rows_even[c, z, pl.ds(k, 1), :], rows_odd[c, z, pl.ds(k, 1), :]
            cells[(c, *at, pl.ds(0, 1), col)] = jnp.where(even, two, one)
            cells[(c, *at, pl.ds(ny - 1, 1), col)] = jnp.where(even, one, two)


def stencil_kernel(step, *refs):
    if step == 0:
        field, base, new, p_lo, p_hi, r_lo, r_hi, slope_ref = refs
    elif step < STEPS - 1:
        field, base, slope_ref, new, p_lo, p_hi, r_lo, r_hi = refs
    else:
        field, base, slope_ref, before, new, p_lo, p_hi, r_lo, r_hi, both = refs
    nz, ny, nx = field.shape[1:]

    def outside(c, yt, k):
        return jnp.zeros((ROWS, LANES), jnp.float32)

    def do(z, lower, upper):
        def at(yt, k):
            return (z, pl.ds(yt * ROWS, ROWS), pl.ds(k * LANES, LANES))

        def beside(ref, there, off):
            return tile_of(ref, (z + off,)) if there else outside

        def put(c, yt, k, value):
            new[(c, *at(yt, k))] = value
            if yt == 0:
                r_lo[c, z, pl.ds(k, 1), :] = value[:1]
            if yt == ny // ROWS - 1:
                r_hi[c, z, pl.ds(k, 1), :] = value[ROWS - 1:]
            if step == STEPS - 1:
                both[(c, *at(yt, k))] = before[(c, *at(yt, k))] + field[(c, *at(yt, k))]

        b_lo, b_hi = beside(base, lower, -1), beside(base, upper, 1)

        def slopes(flows, yt, k):
            if step > 0:
                return [[slope_ref[(3 * i + j, *at(yt, k))] for j in range(3)] for i in range(3)]
            found = []
            for along in (lambda j: flows[j].along_x(yt, k), lambda j: flows[j].along_y(yt, k), lambda j: (b_hi(j, yt, k), b_lo(j, yt, k))):
                sides = [along(j) for j in range(3)]
                found.append([hi - lo for hi, lo in sides])
            return found

        def put_slopes(yt, k, slope):
            for i in range(3):
                for j in range(3):
                    slope_ref[(3 * i + j, *at(yt, k))] = slope[i][j]

        plane(tile_of(field, (z,)), beside(field, lower, -1), beside(field, upper, 1), slopes, tile_of(base, (z,)), put, ny, nx,
              put_slopes if step == 0 else None)

    def body(z, carry):
        do(z, True, True)
        return carry

    do(0, False, True)
    p_lo[...] = new[:, 0]
    lax.fori_loop(1, nz - 1, body, 0)
    do(nz - 1, True, False)
    p_hi[...] = new[:, nz - 1]


def stencil(step, field, base, slopes=None, before=None):
    _, nz, ny, nx = field.shape
    outs = [f32(*field.shape)] + [f32(4, ny, nx)] * 2 + [f32(4, nz, nx // LANES, LANES)] * 2
    args = [field, base]
    if step == 0:
        outs.append(f32(9, nz, ny, nx))
    else:
        args.append(slopes)
    if step == STEPS - 1:
        args.append(before)
        outs.append(f32(*field.shape))
    ins = [IN_VMEM] * len(args)
    return call(functools.partial(stencil_kernel, step), "stencil", outs, ins, [IN_VMEM] * len(outs), cost=FREE)(*args)


def row_fix_kernel(after, p_lo, p_hi, r_lo, r_hi, own_e, own_o, base_e, base_o, far_e, far_o, fbase_e, fbase_o,
                   q_e, q_o, s_e, s_o):
    del after
    nz = r_lo.shape[1]
    uppers = upper_sides("cross")

    def body(z, carry):
        for upper, own, base, far, fbase, s in ((uppers[0], own_e, base_e, far_e, fbase_e, s_e),
                                                (uppers[1], own_o, base_o, far_o, fbase_o, s_o)):
            add = fix(sign_of(upper), 1, [own[c, z] for c in range(3)], [base[4 + c, z] for c in range(3)],
                      [far[c, z] for c in range(4)], [fbase[4 + c, z] for c in range(3)])
            for c in range(4):
                s[c, z] = jnp.where(upper, r_hi[c, z], r_lo[c, z]) + add[c]
        return carry

    lax.fori_loop(0, nz, body, 0)
    for upper, q in zip(upper_sides("span"), (q_e, q_o)):
        for c in range(4):
            q[c] = jnp.where(upper, p_hi[c], p_lo[c])
        put_rows(q, uppers[0], s_e, s_o, jnp.where(upper, nz - 1, 0), ())


def row_fix(after, planes, rows, own_rows, base_rows, far_rows, far_base_rows):
    outs = [f32(*planes[0].shape)] * 2 + [f32(*rows[0].shape)] * 2
    cost = FREE
    return call(row_fix_kernel, "row_fix", outs, [ANYWHERE] + [IN_VMEM] * 12, [IN_VMEM] * 4, cost=cost)(
        after, *planes, *rows, *own_rows, *base_rows, *far_rows, *far_base_rows)


def far_fix_kernel(got_e, got_o, far_e, far_o, fbase_e, fbase_o, old_e, old_o, base_e, base_o, next_e, next_o):
    _, ny, nx = got_e.shape
    span, ends = lax.axis_index("span"), lax.axis_size("span") - 1
    uppers = upper_sides("span")
    sides = (
        (uppers[0], got_e, far_e, fbase_e, old_e, base_e, next_e),
        (uppers[1], got_o, far_o, fbase_o, old_o, base_o, next_o),
    )
    for upper, got, far, fbase, old, base, nxt in sides:
        there = span != jnp.where(upper, ends, 0)
        for yt in range(ny // ROWS):
            for k in range(nx // LANES):
                tile = (pl.ds(yt * ROWS, ROWS), pl.ds(k * LANES, LANES))
                back = fix(-sign_of(upper), 2, [far[(c, *tile)] for c in range(3)], [fbase[(4 + c, *tile)] for c in range(3)],
                           [old[(c, *tile)] for c in range(4)], [base[(4 + c, *tile)] for c in range(3)])
                for c in range(4):
                    nxt[(c, *tile)] = jnp.where(there, got[(c, *tile)] + back[c], 0.0)


def far_fix(got, far, far_base, old, base):
    args = [*got, *far, *far_base, *old, *base]
    return call(far_fix_kernel, "far_fix", [f32(*got[0].shape)] * 2, [IN_VMEM] * len(args), [IN_VMEM] * 2, cost=FREE)(*args)


def plane_fix_kernel(big, q_e, q_o, s_e, s_o, own_e, own_o, base_e, base_o, fbase_e, fbase_o, far_e, far_o,
                     whole, out_e, out_o, row_e, row_o):
    del big
    _, ny, nx = q_e.shape
    nz = s_e.shape[1]
    even_y = is_even("cross")
    uppers = upper_sides("span")
    sides = (
        (uppers[0], q_e, own_e, base_e, fbase_e, far_e, out_e),
        (uppers[1], q_o, own_o, base_o, fbase_o, far_o, out_o),
    )
    row_e[...] = s_e[...]
    row_o[...] = s_o[...]
    for upper, q, own, base, fbase, far, out in sides:
        for yt in range(ny // ROWS):
            for k in range(nx // LANES):
                tile = (pl.ds(yt * ROWS, ROWS), pl.ds(k * LANES, LANES))
                add = fix(sign_of(upper), 2, [own[(c, *tile)] for c in range(3)], [base[(4 + c, *tile)] for c in range(3)],
                          [far[(c, *tile)] for c in range(4)], [fbase[(4 + c, *tile)] for c in range(3)])
                for c in range(4):
                    out[(c, *tile)] = q[(c, *tile)] + add[c]
        z = jnp.where(upper, nz - 1, 0)
        whole[:, z] = out[...]
        for c in range(4):
            for k in range(nx // LANES):
                col = pl.ds(k * LANES, LANES)
                lo, hi = out[c, pl.ds(0, 1), col], out[c, pl.ds(ny - 1, 1), col]
                row_e[c, z, pl.ds(k, 1), :] = jnp.where(even_y, hi, lo)
                row_o[c, z, pl.ds(k, 1), :] = jnp.where(even_y, lo, hi)

    def body(z, carry):
        put_rows(whole, even_y, s_e, s_o, z, (z,))
        return carry

    lax.fori_loop(1, nz - 1, body, 0)


def plane_fix(last, field, planes, rows, own, base, far_base, far):
    outs = [f32(*planes[0].shape)] * 2 + [f32(*rows[0].shape)] * 2
    scratch = []
    if last:
        outs, scratch = [], [VMEM(o.shape, o.dtype) for o in outs]
    outs = [f32(*field.shape)] + outs
    args = [field, *planes, *rows, *own, *base, *far_base, *far]
    return call(plane_fix_kernel, "plane_fix", outs, [IN_VMEM] * len(args), [IN_VMEM] * len(outs), scratch,
                cost=FREE, aliases={0: 0})(*args)


def last_planes_kernel(big, own_e, own_o, base_e, base_o, fbase_e, fbase_o, far_e, far_o, whole):
    nz, ny, nx = big.shape[1:]
    uppers = upper_sides("span")
    for upper, own, base, fbase, far in ((uppers[0], own_e, base_e, fbase_e, far_e), (uppers[1], own_o, base_o, fbase_o, far_o)):
        z = jnp.where(upper, nz - 1, 0)
        for yt in range(ny // ROWS):
            for k in range(nx // LANES):
                tile = (pl.ds(yt * ROWS, ROWS), pl.ds(k * LANES, LANES))
                add = fix(sign_of(upper), 2, [own[(c, *tile)] for c in range(3)], [base[(4 + c, *tile)] for c in range(3)],
                          [far[(c, *tile)] for c in range(4)], [fbase[(4 + c, *tile)] for c in range(3)])
                for c in range(4):
                    whole[(c, z, *tile)] = big[(c, z, *tile)] + add[c]


def last_rows_kernel(big, own_e, own_o, base_e, base_o, far_e, far_o, fbase_e, fbase_o, whole):
    nz, ny, nx = big.shape[1:]
    uppers = upper_sides("cross")

    def body(z, carry):
        adds = []
        for upper, own, base, far, fbase in ((uppers[0], own_e, base_e, far_e, fbase_e), (uppers[1], own_o, base_o, far_o, fbase_o)):
            adds.append(fix(sign_of(upper), 1, [own[c, z] for c in range(3)], [base[4 + c, z] for c in range(3)],
                            [far[c, z] for c in range(4)], [fbase[4 + c, z] for c in range(3)]))
        for c in range(4):
            lo, hi = jnp.where(uppers[0], adds[1][c], adds[0][c]), jnp.where(uppers[0], adds[0][c], adds[1][c])
            for k in range(nx // LANES):
                col = pl.ds(k * LANES, LANES)
                whole[c, z, pl.ds(0, 1), col] = big[c, z, pl.ds(0, 1), col] + lo[k:k + 1]
                whole[c, z, pl.ds(ny - 1, 1), col] = big[c, z, pl.ds(ny - 1, 1), col] + hi[k:k + 1]
        return carry

    lax.fori_loop(0, nz, body, 0)


def in_place(kernel, name, *args):
    return call(kernel, name, f32(*args[0].shape), [IN_VMEM] * len(args), IN_VMEM, cost=FREE, aliases={0: 0})(*args)


def spread_kernel(normals, weights):
    count = normals.shape[1]
    across = jnp.concatenate([normals[...], jnp.zeros((ROWS - 4, count), jnp.float32)]).T
    for c in range(4):
        weights[c] = jnp.broadcast_to(across[:, c:c + 1], (count, LANES)).reshape(count // ROWS, ROWS, LANES)


def spread(normals):
    return call(spread_kernel, "spread", f32(4, normals.shape[1] // ROWS, ROWS, LANES), [IN_VMEM], IN_VMEM, cost=FREE)(normals)


def finish_kernel(field, both, blocks, weights, sections, new, table, rows, sems):
    nz = field.shape[1]

    def out(z):
        return pltpu.make_async_copy(field.at[:, z], new.at[:, z], sems.at[z])

    for z in range(nz):
        out(z).start()
    gather_tiles((both, field), blocks, weights, rows)
    labels = lax.broadcasted_iota(jnp.int32, (table.shape[0], rows.shape[0]), 0)
    onehot = (labels == sections[...]).astype(jnp.float32).astype(jnp.bfloat16)
    left, parts = rows[...], []
    for _ in range(3):
        parts.append(left.astype(jnp.bfloat16))
        left = left - parts[-1].astype(jnp.float32)
    sums = jnp.dot(onehot, jnp.concatenate(parts, axis=1), preferred_element_type=jnp.float32)
    table[...] = sums[:, :LANES] + sums[:, LANES:2 * LANES] + sums[:, 2 * LANES:]
    for z in range(nz):
        out(z).wait()


def finish(field, both, blocks, weights, sections, total):
    scratch = [VMEM((blocks.shape[0], LANES), jnp.float32), pltpu.SemaphoreType.DMA((field.shape[1],))]
    return call(finish_kernel, "finish", [f32(*field.shape), f32(total, LANES)],
                [IN_VMEM] * 2 + [IN_SMEM] + [IN_VMEM] * 2, [ANYWHERE, IN_VMEM], scratch)(
        field, both, blocks, weights, sections)


def swap(sides, axis):
    even, odd = sides
    count = lax.axis_size(axis)
    return [lax.ppermute(even, axis, [(i, i ^ 1) for i in range(count)]),
            lax.ppermute(odd, axis, [(i, ((i + 1) ^ 1) - 1) for i in range(1, count - 1)])]


def local(adjoint_start, base_flow, wall_blocks, tile_sections, tile_normals, modes):
    sides = outer_sides(adjoint_start, base_flow)
    own = base_planes = sides[:2]
    own_rows = base_rows = sides[2:]
    far_rows = far_base_rows = swap(base_rows, "cross")
    far = far_base = swap(base_planes, "span")
    field, before, slopes, both = adjoint_start, None, None, None
    old, got, after = None, None, base_planes[0]
    for step in range(STEPS):
        fresh, *edge = stencil(step, field, base_flow, slopes, before)
        if step == 0:
            slopes = edge.pop()
        else:
            far = far_fix(got, far, far_base, old, base_planes)
            after = far[0]
            if step == STEPS - 1:
                both = edge.pop()
                field = in_place(last_planes_kernel, "last_planes", fresh, *own, *base_planes, *far_base, *far)
                field = in_place(last_rows_kernel, "last_rows", field, *own_rows, *base_rows, *far_rows, *far_base_rows)
                break
        *planes, row_lo, row_hi = row_fix(after, edge[:2], edge[2:], own_rows, base_rows, far_rows, far_base_rows)
        if step < STEPS - 1:
            got = swap(planes, "span")
        before, old = field, own
        field, *out = plane_fix(step == STEPS - 1, fresh, planes, (row_lo, row_hi), own, base_planes, far_base, far)
        own, own_rows = out[:2], out[2:]
        if step < STEPS - 1:
            far_rows = swap(own_rows, "cross")
    sections = tile_sections.reshape(1, -1)
    devices = lax.axis_size("cross") * lax.axis_size("span")
    field, table = finish(field, both, wall_blocks, spread(tile_normals), sections, devices * SEC_DEV)
    parts = lax.all_to_all(table.reshape(devices, SEC_DEV, LANES), ("span", "cross"), 0, 0, tiled=True)
    section_sum = jnp.sum(parts, axis=0)
    modal_load = jnp.dot(section_sum, modes, precision=lax.Precision.HIGHEST, preferred_element_type=jnp.float32)
    return field, modal_load


def solution(mesh):
    placed = (
        P(None, "span", "cross", None),
        P(None, "span", "cross", None),
        P(("span", "cross")),
        P(("span", "cross"), None),
        P(None, ("span", "cross")),
        P(),
    )
    return jax.shard_map(
        local,
        mesh=mesh,
        in_specs=placed,
        out_specs=(P(None, "span", "cross", None), P(("span", "cross"), None)),
        check_vma=False,
    )
```
